512 devices in a mesh: rep: 2 (over core), dp: 32 (over y, x), tensor: 8 (over z).
Axes of the slice: x: 4, y: 8, z: 8, core: 2. Of those that a mesh axis runs over, the one named last changes fastest.
Arguments:
- queries: bfloat16 [2, 4096, 4096], P('rep', 'dp', 'tensor'), may hold values from -100 to 100
- passages: bfloat16 [2, 4096, 4096], P('rep', 'dp', 'tensor'), may hold values from -100 to 100
- positives: int32 [2, 4096], P('rep', 'dp'), may hold values from 0 to 4095, each once within a row
- hidden_rows: bfloat16 [2, 4096, 14336], P('rep', 'dp', 'tensor'), may hold values from -6 to 6
- sketch: float32 [4096, 32], P('tensor'), may hold values from -6 to 6
Outputs:
- grad_queries: bfloat16 [2, 4096, 4096], P('rep', 'dp', 'tensor')
- grad_passages: bfloat16 [2, 4096, 4096], P('rep', 'dp', 'tensor')
- p_factor: float32 [14336, 32], P('tensor')
- q_factor: float32 [4096, 32], P('tensor')
The draws below stay inside these ranges and needn't reach their ends.
All inputs are finite; a program needn't handle non-finite values.
Results may differ from the reference program's by a relative error of at most 0.025.
Values may be sent and summed in bfloat16 or wider, within the bound.
No kernel may reach another device: no remote copies, remote signals or barrier semaphores. Data moves between devices by JAX's collectives and lax.ppermute only.
A program may use at most 128 MiB of HBM per device.

```python
import math
import jax
import jax.numpy as jnp
from jax import lax

D = 4096
FF = 14336
RANK = 32
LEVELS = 7
ROWS = 128
GROUPS = 2
GROUP = 4096
BATCH = 8192


PASSAGE_SCALE = 0.5


PASSAGE_LIFT = 4.0


def pair_base(key):
    first = jax.random.fold_in(key, 0)
    second = jax.random.fold_in(key, 1)
    fifth = jax.random.fold_in(key, 4)
    shape = (GROUPS, GROUP, D)
    query_base = jnp.clip(jax.random.normal(first, shape, jnp.float32), -6.0, 6.0)
    passage_base = jnp.clip(jax.random.normal(second, shape, jnp.float32), -6.0, 6.0)
    offset = jnp.clip(jax.random.normal(fifth, (GROUPS, 1, D), jnp.float32), -2.5, 2.5)
    return (query_base, passage_base, offset)


def upper_half(offset):
    column = jnp.arange(D)
    return offset * (column >= D // 2).astype(jnp.float32)[None, None, :]


def draw_queries(key, part):
    query_base, passage_base, offset = pair_base(key)
    return (0.22 * (query_base + 2.0 * offset)).astype(jnp.bfloat16)


def draw_passages(key, part):
    query_base, passage_base, offset = pair_base(key)
    return (PASSAGE_SCALE * (passage_base + PASSAGE_LIFT * upper_half(offset))).astype(jnp.bfloat16)


def block_scale(rng, shape, pieces, least, high):
    def one(dim, blocks):
        steps = jax.random.uniform(jax.random.fold_in(jax.random.fold_in(rng, 6), dim), (blocks,), jnp.float32, least / len(pieces), high / len(pieces))
        return jnp.repeat(jnp.exp(steps), shape[dim] // blocks).reshape((-1,) + (1,) * (len(shape) - dim - 1))

    loudness = one(*pieces[0])
    for cut in pieces[1:]:
        loudness = loudness * one(*cut)
    return loudness


def gaussian(rng, extent, scale, most, cuts=(), kind=jnp.bfloat16):
    drawn = scale * jax.random.normal(rng, extent, jnp.float32)
    if cuts:
        drawn = drawn * block_scale(rng, extent, cuts, -0.22, 0.18)
    return jnp.clip(drawn, -most, most).astype(kind)


def setup_inputs(seed: int = 0) -> dict:
    splits = jax.random.split(jax.random.key(seed), 6)
    return {
        "queries": draw_queries(jax.random.fold_in(splits[5], 71), 0),
        "passages": draw_passages(jax.random.fold_in(splits[5], 71), 0),
        "positives": jax.vmap(lambda own: jax.random.permutation(own, GROUP))(jax.random.split(splits[2], GROUPS)).reshape((GROUPS, GROUP)).astype(jnp.int32),
        "hidden_rows": gaussian(splits[3], (GROUPS, GROUP, FF), 1.0, 6.0, ((0, 2), (1, 32), (2, 8))),
        "sketch": gaussian(splits[4], (D, RANK), 1.0, 6.0, ((0, 8),), jnp.float32),
    }


SOFTMAX_TEMP = 4.0

def level_gradient(raw_sum, nesting_width, targets):
    nesting_scale = SOFTMAX_TEMP / math.sqrt(nesting_width)
    logits = nesting_scale * raw_sum
    shifted = logits - lax.optimization_barrier(jnp.max(logits, axis=1, keepdims=True))
    exponent = jnp.exp(shifted)
    softmax_rows = exponent / lax.optimization_barrier(jnp.sum(exponent, axis=1, keepdims=True))
    return nesting_scale * (softmax_rows - targets)

def device_rounded(coefficient, query_cols):

    def add_device(device, total):
        start = device * ROWS
        coef_rows = lax.dynamic_slice_in_dim(coefficient, start, ROWS, 0)
        query_part = lax.dynamic_slice_in_dim(query_cols, start, ROWS, 0)
        term = jnp.dot(coef_rows.T, query_part, precision=lax.Precision.HIGHEST)
        return total + term.astype(jnp.bfloat16).astype(jnp.float32)
    return lax.fori_loop(0, GROUP // ROWS, add_device, jnp.zeros((GROUP, query_cols.shape[1]), jnp.float32))

def group_gradients(query_group, passage_cluster, positive_group):
    query_full = query_group.astype(jnp.float32)
    passage_full = passage_cluster.astype(jnp.float32)
    targets = (jnp.arange(GROUP, dtype=jnp.int32)[None, :] == positive_group[:, None]).astype(jnp.float32)
    bounds = [D >> level for level in range(LEVELS)] + [0]
    running = jnp.zeros((GROUP, GROUP), jnp.float32)
    level_grads = [None] * LEVELS
    for level in reversed(range(LEVELS)):
        upper = bounds[level]
        lower_edge = bounds[level + 1]
        running = running + jnp.dot(query_full[:, lower_edge:upper], passage_full[:, lower_edge:upper].T, precision=lax.Precision.HIGHEST)
        level_grads[level] = level_gradient(running, upper, targets)
    query_parts = []
    passage_parts = []
    combined = jnp.zeros((GROUP, GROUP), jnp.float32)
    for level in range(LEVELS):
        combined = combined + level_grads[level]
        coefficient = combined.astype(jnp.bfloat16).astype(jnp.float32)
        upper = bounds[level]
        lower_edge = bounds[level + 1]
        query_parts.append(jnp.dot(coefficient, passage_full[:, lower_edge:upper], precision=lax.Precision.HIGHEST))
        passage_parts.append(device_rounded(coefficient, query_full[:, lower_edge:upper]))
    grad_query = jnp.concatenate(query_parts[::-1], axis=1).astype(jnp.bfloat16)
    grad_passage = jnp.concatenate(passage_parts[::-1], axis=1).astype(jnp.bfloat16)
    return (grad_query, grad_passage)

def reference(queries, passages, positives, hidden_rows, sketch):
    query_list = []
    passage_list = []
    for group_index in range(GROUPS):
        grad_query, grad_passage = group_gradients(queries[group_index], passages[group_index], positives[group_index])
        query_list.append(grad_query)
        passage_list.append(grad_passage)
    grad_queries = jnp.stack(query_list)
    grad_passages = jnp.stack(passage_list)
    cotangent = grad_queries.reshape(BATCH, D).astype(jnp.float32)
    hidden_full = hidden_rows.reshape(BATCH, FF).astype(jnp.float32)
    sketched = jnp.dot(cotangent, sketch, precision=lax.Precision.HIGHEST) / BATCH
    p_sum = jnp.dot(hidden_full.T, sketched, precision=lax.Precision.HIGHEST)
    gram = jnp.dot(p_sum.T, p_sum, precision=lax.Precision.HIGHEST)
    lower = jnp.linalg.cholesky(gram)
    p_factor = lax.linalg.triangular_solve(lower, p_sum, left_side=False, lower=True, transpose_a=True)
    projected = jnp.dot(hidden_full, p_factor, precision=lax.Precision.HIGHEST)
    q_factor = jnp.dot(cotangent.T, projected, precision=lax.Precision.HIGHEST) / BATCH
    return (grad_queries, grad_passages, p_factor, q_factor)
```

```python
import functools
import math

import jax
import jax.numpy as jnp
from jax import lax
from jax.experimental import pallas as pl
from jax.experimental.pallas import tpu as pltpu
from jax.sharding import Mesh, PartitionSpec as P

LEVELS = 7
SOFTMAX_TEMP = 4.0
NY = 8
NX = 4
NZ = 8
LANES = 128
f32 = jnp.float32
bf16 = jnp.bfloat16
HIGHEST = lax.Precision.HIGHEST
VMEM = pl.BlockSpec(memory_space=pltpu.VMEM)
ALL_ROWS = ("rep", "y", "xh", "xl")
NT = (((1,), (1,)), ((), ()))
TN = (((0,), (0,)), ((), ()))


def scale_of(level, full):
    return SOFTMAX_TEMP / math.sqrt(full >> level)


def swap(blocks, axes):
    return lax.all_to_all(blocks, axes, 0, 0, tiled=True)


def share(block, axes, count):
    return swap(jnp.broadcast_to(block[None], (count,) + block.shape), axes)


def scores_kernel(q_ref, p_ref, e_ref, stats_ref):
    chunks, rows, width = q_ref.shape
    full = chunks * width
    cols = p_ref.shape[1]
    lane = lax.broadcasted_iota(jnp.int32, (rows, LANES), 1)
    table = jnp.where(lane == 8 + LEVELS, 1.0, 0.0).astype(f32)

    def dot(q, p):
        return lax.dot_general(q, p, NT, preferred_element_type=f32)

    def finish(level, raw, table):
        logits = scale_of(level, full) * raw
        top = jnp.max(logits, axis=1, keepdims=True)
        e = jnp.exp(logits - top)
        e_ref[level] = e
        total = jnp.sum(e, axis=1, keepdims=True)
        table = jnp.where(lane == level, top, table)
        return jnp.where(lane == 8 + level, total, table)

    raw = None
    for level in reversed(range(LEVELS)):
        upper = full >> level
        lower = full >> (level + 1) if level + 1 < LEVELS else 0
        if upper < LANES:
            q = q_ref[0, :, :LANES]
            q = jnp.where(lane < upper, q, jnp.zeros_like(q))
            part = dot(q, p_ref[0, :, :LANES])
            table = finish(level, part, table)
            continue
        if upper == LANES:
            raw = dot(q_ref[0, :, :LANES], p_ref[0, :, :LANES])
        elif upper <= width:
            raw = raw + dot(q_ref[0, :, lower:upper], p_ref[0, :, lower:upper])
        else:
            parts = [dot(q_ref[c], p_ref[c]) for c in range(lower // width, upper // width)]
            while len(parts) > 1:
                parts = [a + b for a, b in zip(parts[::2], parts[1::2])]
            raw = raw + parts[0]
        table = finish(level, raw, table)
    stats_ref[...] = table.T[:16]


def grads_kernel(q_ref, p_ref, e_ref, stats_ref, all_ref, pos_ref, s_ref, gq_ref, gp_ref, sk_ref):
    chunks, rows, width = q_ref.shape
    full = chunks * width
    cols = p_ref.shape[1]
    top = all_ref[0, :8]
    for src in range(1, all_ref.shape[0]):
        top = jnp.maximum(top, all_ref[src, :8])
    total = all_ref[0, 8:] * jnp.exp(all_ref[0, :8] - top)
    for src in range(1, all_ref.shape[0]):
        total = total + all_ref[src, 8:] * jnp.exp(all_ref[src, :8] - top)
    factor = jnp.exp(stats_ref[:8] - top) / total
    place = jnp.broadcast_to(pos_ref[...].astype(f32), (8, rows))
    table = jnp.concatenate([factor, place, jnp.zeros((LANES - 16, rows), f32)], axis=0).T
    column = lax.broadcasted_iota(jnp.int32, (rows, cols), 1).astype(f32)
    target = (column == table[:, 8:9]).astype(f32)
    coef = jnp.zeros((rows, cols), f32)
    sketched = jnp.zeros(sk_ref.shape, f32)
    lane = lax.broadcasted_iota(jnp.int32, (1, LANES), 1)

    def put(chunk, low, high, gq, gp, sketched):
        gq_ref[chunk, :, low:high] = gq.astype(bf16)
        gp_ref[chunk, :, low:high] = gp.astype(bf16)
        return sketched + lax.dot_general(
            s_ref[chunk, :, low:high], gq, NT, precision=HIGHEST, preferred_element_type=f32
        )

    def both(c, chunk, low, high):
        gq = jnp.dot(c, p_ref[chunk, :, low:high], preferred_element_type=f32)
        gp = lax.dot_general(c, q_ref[chunk, :, low:high], TN, preferred_element_type=f32)
        return gq, gp

    held = None
    for level in range(LEVELS):
        scale = scale_of(level, full)
        grad = scale * (e_ref[level] * table[:, level:level + 1] - target)
        coef = coef + grad
        c = coef.astype(bf16)
        upper = full >> level
        lower = full >> (level + 1) if level + 1 < LEVELS else 0
        if upper > width:
            for chunk in range(lower // width, upper // width):
                gq, gp = both(c, chunk, 0, width)
                sketched = put(chunk, 0, width, gq, gp, sketched)
        elif lower >= LANES:
            gq, gp = both(c, 0, lower, upper)
            sketched = put(0, lower, upper, gq, gp, sketched)
        else:
            gq, gp = both(c, 0, 0, LANES)
            if held is None:
                held = (gq, gp)
            else:
                gq = jnp.where(lane < upper, gq, held[0])
                gp = jnp.where(lane < upper, gp, held[1])
                sketched = put(0, 0, LANES, gq, gp, sketched)
    sk_ref[...] = sketched


def exact_dot(wide, narrow, dims):
    hi = wide.astype(bf16)
    rest = wide - hi.astype(f32)
    mid = rest.astype(bf16)
    lo = (rest - mid.astype(f32)).astype(bf16)
    terms = [lax.dot_general(t, narrow, dims, preferred_element_type=f32) for t in (lo, mid, hi)]
    return terms[0] + terms[1] + terms[2]


def sum_all(value):
    rows = value.shape[0]
    count = 2 * NY * NX
    landed = swap(value.reshape(count, rows // count, LANES), ALL_ROWS)
    return share(jnp.sum(landed, axis=0), ALL_ROWS, count).reshape(rows, LANES)


def body(queries, passages, positives, hidden_rows, sketch):
    q = queries[0]
    p = passages[0]
    rows, width = q.shape
    full = width * NZ
    rank = sketch.shape[1]
    xh = lax.axis_index("xh")
    xl = lax.axis_index("xl")
    zi = lax.axis_index("z")
    flip = [(0, 1), (1, 0)]

    q_other = lax.ppermute(q, "xl", flip)
    pos_other = lax.ppermute(positives, "xl", flip)
    q_pair = jnp.concatenate(
        [jnp.where(xl == 0, q, q_other), jnp.where(xl == 0, q_other, q)], axis=0
    )
    pos_pair = jnp.concatenate(
        [jnp.where(xl == 0, positives, pos_other), jnp.where(xl == 0, pos_other, positives)], axis=1
    )
    q_tile = lax.all_gather(q_pair, "z")

    turn = [(a * NZ + b, b * NZ + a) for a in range(NY) for b in range(NZ)]
    turn_far = [
        ((a * 2 + h) * NZ + b, (b * 2 + 1 - h) * NZ + a)
        for a in range(NY) for h in range(2) for b in range(NZ)
    ]
    p_near = lax.ppermute(p, ("y", "z"), turn)
    p_far = lax.ppermute(p, ("y", "xh", "z"), turn_far)
    p_pair = jnp.concatenate([p_near, p_far], axis=0)
    p_tile = share(p_pair, "y", NY)

    s_all = lax.all_gather(sketch.T, "z")

    tile = 2 * rows
    e, stats = pl.pallas_call(
        scores_kernel,
        out_shape=(
            jax.ShapeDtypeStruct((LEVELS, tile, tile), f32),
            jax.ShapeDtypeStruct((16, tile), f32),
        ),
        in_specs=[VMEM, VMEM],
        out_specs=(VMEM, VMEM),
        compiler_params=pltpu.CompilerParams(vmem_limit_bytes=40 << 20),
        name="scores",
    )(q_tile, p_tile)
    stats_all = share(stats, ("xl", "z"), 2 * NZ)

    own_y = pos_pair // (rows * NX)
    own_x = pos_pair // rows % NX
    inside = (own_y == zi) & (own_x % 2 == xl)
    local = jnp.where(inside, pos_pair % rows + jnp.where(own_x // 2 == xh, 0, rows), -1)

    gq_part, gp_part, sk_part = pl.pallas_call(
        grads_kernel,
        out_shape=(
            jax.ShapeDtypeStruct((NZ, tile, width), bf16),
            jax.ShapeDtypeStruct((NY, tile, width), bf16),
            jax.ShapeDtypeStruct((rank, tile), f32),
        ),
        in_specs=[VMEM] * 7,
        out_specs=(VMEM, VMEM, VMEM),
        compiler_params=pltpu.CompilerParams(vmem_limit_bytes=56 << 20),
        name="grads",
    )(q_tile, p_tile, e, stats, stats_all, local, s_all)

    sk_blocks = jnp.stack([sk_part[:, :rows], sk_part[:, rows:]])
    sk_blocks = jnp.broadcast_to(sk_blocks[:, None], (2, NZ, rank, rows))
    sk_landed = swap(sk_blocks.reshape(2 * NZ, rank, rows), ("xl", "z"))
    batch = rows * NX * NY * 2
    sketched = jnp.sum(sk_landed, axis=0) / batch

    gq_part, gp_part, sketched = lax.optimization_barrier((gq_part, gp_part, sketched))

    gp_sum = lax.psum_scatter(gp_part, "y", scatter_dimension=0)
    gp_far = lax.ppermute(gp_sum[rows:], "xh", flip)
    gp_own = (gp_sum[:rows].astype(f32) + gp_far.astype(f32)).astype(bf16)
    grad_passages = lax.ppermute(gp_own, ("y", "z"), turn)

    gq_sum = jnp.sum(swap(gq_part, "z").astype(f32), axis=0)
    mine = jnp.where(xl == 0, gq_sum[:rows], gq_sum[rows:])
    other = jnp.where(xl == 0, gq_sum[rows:], gq_sum[:rows])
    grad_queries = (mine + lax.ppermute(other, "xl", flip)).astype(bf16)

    hidden = hidden_rows[0]
    units = hidden.shape[1]
    tiles = units // LANES
    padded = -(-tiles // 2) * 2 + (2 if tiles % 4 else 0)
    p_local = exact_dot(sketched, hidden, (((1,), (0,)), ((), ())))
    flat = p_local.reshape(rank, tiles, LANES).transpose(1, 0, 2).reshape(tiles * rank, LANES)
    pad = padded * rank - tiles * rank
    flat = jnp.concatenate([flat, jnp.zeros((pad, LANES), f32)], axis=0)
    p_flat = sum_all(flat)[:tiles * rank]
    p_sum = p_flat.reshape(tiles, rank, LANES).transpose(1, 0, 2).reshape(rank, units)
    gram_part = lax.dot_general(p_sum, p_sum, NT, precision=HIGHEST)
    proj_part = exact_dot(p_sum, hidden, NT)
    joined = jnp.concatenate(
        [proj_part, jnp.pad(gram_part, ((0, 0), (0, LANES - rank)))], axis=0
    )
    joined = jnp.sum(share(joined, "z", NZ), axis=0)
    proj = joined[:rank]
    gram = joined[rank:, :rank]

    q_local = exact_dot(proj, grad_queries, (((1,), (0,)), ((), ())))
    q_flat = q_local.reshape(rank, width // LANES, LANES).transpose(1, 0, 2).reshape(-1, LANES)
    q_sum = sum_all(q_flat).reshape(width // LANES, rank, LANES).transpose(1, 0, 2)
    q_sum = q_sum.reshape(rank, width)

    lower = jnp.linalg.cholesky(gram)
    inverse = lax.linalg.triangular_solve(
        lower, jnp.eye(rank, dtype=f32), left_side=True, lower=True
    )
    p_factor = lax.dot_general(p_sum, inverse, (((0,), (1,)), ((), ())), precision=HIGHEST)
    q_factor = lax.dot_general(q_sum, inverse, (((0,), (1,)), ((), ())), precision=HIGHEST) / batch
    return (grad_queries[None], grad_passages[None], p_factor, q_factor)


def solution(mesh):
    grid = Mesh(mesh.devices.reshape(2, NY, 2, 2, NZ), ("rep", "y", "xh", "xl", "z"))
    dp = ("y", "xh", "xl")
    placed = (
        P("rep", dp, "z"),
        P("rep", dp, "z"),
        P("rep", dp),
        P("rep", dp, "z"),
        P("z", None),
    )
    return jax.shard_map(
        body,
        mesh=grid,
        in_specs=placed,
        out_specs=(P("rep", dp, "z"), P("rep", dp, "z"), P("z", None), P("z", None)),
        check_vma=False,
    )
```

```python
import math

import jax
import jax.numpy as jnp
from jax import lax
from jax.experimental import pallas as pl
from jax.experimental.pallas import tpu as pltpu
from jax.sharding import Mesh, PartitionSpec as P

LEVELS = 7
SOFTMAX_TEMP = 4.0
NY = 8
NX = 4
NZ = 8
LANES = 128
f32 = jnp.float32
bf16 = jnp.bfloat16
HIGHEST = lax.Precision.HIGHEST
VMEM = pl.BlockSpec(memory_space=pltpu.VMEM)
ALL_ROWS = ("rep", "y", "xh", "xl")
NT = (((1,), (1,)), ((), ()))
TN = (((0,), (0,)), ((), ()))


def scale_of(level, full):
    return SOFTMAX_TEMP / math.sqrt(full >> level)


def swap(blocks, axes):
    return lax.all_to_all(blocks, axes, 0, 0, tiled=True)


def share(block, axes, count):
    return swap(jnp.broadcast_to(block[None], (count,) + block.shape), axes)


def scores_kernel(q_ref, raw_p_ref, e_ref, stats_ref, p_ref):
    chunks, rows, width = q_ref.shape
    full = chunks * width
    piece = raw_p_ref.shape[2]
    lane = lax.broadcasted_iota(jnp.int32, (rows, LANES), 1)
    table = jnp.where(lane == 8 + LEVELS, 1.0, 0.0).astype(f32)

    for y in range(raw_p_ref.shape[0]):
        for half in range(2):
            place = (2 * y + half) * piece
            for chunk in range(chunks):
                p_ref[chunk, place:place + piece] = raw_p_ref[y, half * chunks + chunk]

    def dot(q, p):
        return lax.dot_general(q, p, NT, preferred_element_type=f32)

    def finish(level, raw, table):
        logits = scale_of(level, full) * raw
        top = jnp.max(logits, axis=1, keepdims=True)
        e = jnp.exp(logits - top)
        e_ref[level] = e
        total = jnp.sum(e, axis=1, keepdims=True)
        table = jnp.where(lane == level, top, table)
        return jnp.where(lane == 8 + level, total, table)

    raw = None
    for level in reversed(range(LEVELS)):
        upper = full >> level
        lower = full >> (level + 1) if level + 1 < LEVELS else 0
        if upper < LANES:
            q = q_ref[0, :, :LANES]
            q = jnp.where(lane < upper, q, jnp.zeros_like(q))
            table = finish(level, dot(q, p_ref[0, :, :LANES]), table)
            continue
        if upper == LANES:
            raw = dot(q_ref[0, :, :LANES], p_ref[0, :, :LANES])
        elif upper <= width:
            raw = raw + dot(q_ref[0, :, lower:upper], p_ref[0, :, lower:upper])
        else:
            parts = [dot(q_ref[c], p_ref[c]) for c in range(lower // width, upper // width)]
            while len(parts) > 1:
                parts = [a + b for a, b in zip(parts[::2], parts[1::2])]
            raw = raw + parts[0]
        table = finish(level, raw, table)
    stats_ref[...] = table.T[:16]


def three_terms(value):
    hi = value.astype(bf16)
    rest = value - hi.astype(f32)
    mid = rest.astype(bf16)
    return hi, mid, (rest - mid.astype(f32)).astype(bf16)


def grads_kernel(
    at_ref, q_ref, p_ref, e_ref, stats_ref, all_ref, pos_ref, s_ref, gq_ref, gp_ref, sk_ref
):
    chunks, rows, width = q_ref.shape
    full = chunks * width
    cols = p_ref.shape[1]
    rank = s_ref.shape[1]
    piece = gp_ref.shape[2]
    top = all_ref[0, :8]
    for src in range(1, all_ref.shape[0]):
        top = jnp.maximum(top, all_ref[src, :8])
    total = all_ref[0, 8:] * jnp.exp(all_ref[0, :8] - top)
    for src in range(1, all_ref.shape[0]):
        total = total + all_ref[src, 8:] * jnp.exp(all_ref[src, :8] - top)
    factor = jnp.exp(stats_ref[:8] - top) / total
    place = jnp.broadcast_to(pos_ref[...].astype(f32), (8, rows))
    table = jnp.concatenate([factor, place, jnp.zeros((LANES - 16, rows), f32)], axis=0).T
    column = lax.broadcasted_iota(jnp.int32, (rows, cols), 1).astype(f32)
    target = (column == table[:, 8:9]).astype(f32)
    coef = jnp.zeros((rows, cols), f32)
    lane = lax.broadcasted_iota(jnp.int32, (1, LANES), 1)
    sk_ref[...] = jnp.zeros(sk_ref.shape, f32)

    def put(chunk, low, high, gq, gp):
        gq_hi = gq.astype(bf16)
        gq_ref[chunk, :, low:high] = gq_hi
        gp = gp.astype(bf16)
        for part in range(rows // piece):
            gp_ref[part // 2, part % 2 * chunks + chunk, :, low:high] = gp[
                part * piece:(part + 1) * piece
            ]
        gq_lo = (gq - gq_hi.astype(f32)).astype(bf16)
        terms = three_terms(s_ref[(at_ref[0] + chunks - chunk) % chunks, :, low:high])
        big = lax.dot_general(
            jnp.concatenate(terms, axis=0), gq_hi, NT, preferred_element_type=f32
        )
        low_part = lax.dot_general(
            jnp.concatenate(terms[:2], axis=0), gq_lo, NT, preferred_element_type=f32
        )
        small = big[2 * rank:] + low_part[rank:]
        sk_ref[...] += small + (big[rank:2 * rank] + low_part[:rank]) + big[:rank]

    def both(c, chunk, low, high):
        gq = jnp.dot(c, p_ref[chunk, :, low:high], preferred_element_type=f32)
        gp = lax.dot_general(c, q_ref[chunk, :, low:high], TN, preferred_element_type=f32)
        return gq, gp

    held = None
    for level in range(LEVELS):
        scale = scale_of(level, full)
        grad = scale * (e_ref[level] * table[:, level:level + 1] - target)
        coef = coef + grad
        c = coef.astype(bf16)
        upper = full >> level
        lower = full >> (level + 1) if level + 1 < LEVELS else 0
        if upper > width:
            for chunk in range(lower // width, upper // width):
                put(chunk, 0, width, *both(c, chunk, 0, width))
        elif lower >= LANES:
            put(0, lower, upper, *both(c, 0, lower, upper))
        else:
            gq, gp = both(c, 0, 0, LANES)
            if held is None:
                held = (gq, gp)
            else:
                gq = jnp.where(lane < upper, gq, held[0])
                gp = jnp.where(lane < upper, gp, held[1])
                put(0, 0, LANES, gq, gp)


def exact_dot(wide, narrow, dims):
    hi, mid, lo = [
        lax.dot_general(t, narrow, dims, preferred_element_type=f32) for t in three_terms(wide)
    ]
    return (lo + mid) + hi


def sum_all(value):
    rows = value.shape[0]
    count = 2 * NY * NX
    landed = swap(value.reshape(count, rows // count, LANES), ALL_ROWS)
    return share(jnp.sum(landed, axis=0), ALL_ROWS, count).reshape(rows, LANES)


def body(queries, passages, positives, hidden_rows, sketch):
    q = queries[0]
    p = passages[0]
    rows, width = q.shape
    full = width * NZ
    rank = sketch.shape[1]
    xl = lax.axis_index("xl")
    zi = lax.axis_index("z")
    flip = [(0, 1), (1, 0)]

    piece = rows // NZ
    p_cut = jnp.broadcast_to(p.reshape(1, NZ, piece, width), (2, NZ, piece, width))
    p_cut = swap(p_cut.reshape(2 * NZ, piece, width), ("xh", "z"))
    p_raw = lax.all_gather(p_cut, "y")

    q_other = lax.ppermute(q, "xl", flip)
    pos_other = lax.ppermute(positives, "xl", flip)
    q_pair = jnp.concatenate(
        [jnp.where(xl == 0, q, q_other), jnp.where(xl == 0, q_other, q)], axis=0
    )
    pos_pair = jnp.concatenate(
        [jnp.where(xl == 0, positives, pos_other), jnp.where(xl == 0, pos_other, positives)], axis=1
    )
    q_tile = share(q_pair, "z", NZ)

    s_own, p_cut = lax.optimization_barrier((sketch.T, p_cut))
    s_all = jnp.stack(
        [s_own]
        + [
            lax.ppermute(s_own, "z", [(i, (i + k) % NZ) for i in range(NZ)])
            for k in range(1, NZ)
        ]
    )
    q_tile, p_raw, s_all = lax.optimization_barrier((q_tile, p_raw, s_all))

    tile = 2 * rows
    e, stats, p_tile = pl.pallas_call(
        scores_kernel,
        out_shape=(
            jax.ShapeDtypeStruct((LEVELS, tile, tile), f32),
            jax.ShapeDtypeStruct((16, tile), f32),
            jax.ShapeDtypeStruct((NZ, tile, width), bf16),
        ),
        in_specs=[VMEM, VMEM],
        out_specs=(VMEM, VMEM, VMEM),
        compiler_params=pltpu.CompilerParams(vmem_limit_bytes=40 << 20),
        name="scores",
    )(q_tile, p_raw)
    stats_all = share(stats, ("xl", "z"), 2 * NZ)

    own_y = pos_pair // (rows * NX)
    own_x = pos_pair // rows % NX
    inside = (own_x % 2 == xl) & (pos_pair % rows // piece == zi)
    local = (own_y * 2 + own_x // 2) * piece + pos_pair % piece
    local = jnp.where(inside, local, -1)

    gq_part, gp_part, sk_part = pl.pallas_call(
        grads_kernel,
        out_shape=(
            jax.ShapeDtypeStruct((NZ, tile, width), bf16),
            jax.ShapeDtypeStruct((NY, 2 * NZ, piece, width), bf16),
            jax.ShapeDtypeStruct((rank, tile), f32),
        ),
        in_specs=[pl.BlockSpec(memory_space=pltpu.SMEM)] + [VMEM] * 7,
        out_specs=(VMEM, VMEM, VMEM),
        compiler_params=pltpu.CompilerParams(vmem_limit_bytes=56 << 20),
        name="grads",
    )(zi.astype(jnp.int32).reshape(1), q_tile, p_tile, e, stats, stats_all, local, s_all)

    gq_sum = lax.psum_scatter(gq_part, "z", scatter_dimension=0)
    mine = jnp.where(xl == 0, gq_sum[:rows], gq_sum[rows:])
    other = jnp.where(xl == 0, gq_sum[rows:], gq_sum[:rows])
    other = lax.ppermute(other, "xl", flip)
    grad_queries = (mine.astype(f32) + other.astype(f32)).astype(bf16)

    gp_sum = lax.psum_scatter(gp_part, "y", scatter_dimension=0)
    gp_home = swap(gp_sum, ("xh", "z")).reshape(2, rows, width).astype(f32)
    grad_passages = (gp_home[0] + gp_home[1]).astype(bf16)

    sk_blocks = jnp.stack([sk_part[:, :rows], sk_part[:, rows:]])
    sk_blocks = jnp.broadcast_to(sk_blocks[:, None], (2, NZ, rank, rows))
    sk_landed = swap(sk_blocks.reshape(2 * NZ, rank, rows), ("xl", "z"))
    batch = rows * NX * NY * 2
    sketched = jnp.sum(sk_landed, axis=0) / batch

    hidden = hidden_rows[0]
    units = hidden.shape[1]
    tiles = units // LANES
    padded = -(-tiles // 2) * 2 + (2 if tiles % 4 else 0)
    p_local = exact_dot(sketched, hidden, (((1,), (0,)), ((), ())))
    flat = p_local.reshape(rank, tiles, LANES).transpose(1, 0, 2).reshape(tiles * rank, LANES)
    pad = padded * rank - tiles * rank
    flat = jnp.concatenate([flat, jnp.zeros((pad, LANES), f32)], axis=0)
    p_flat = sum_all(flat)[:tiles * rank]
    p_sum = p_flat.reshape(tiles, rank, LANES).transpose(1, 0, 2).reshape(rank, units)
    gram_part = lax.dot_general(p_sum, p_sum, NT, precision=HIGHEST)
    proj_part = exact_dot(p_sum, hidden, NT)
    joined = jnp.concatenate(
        [proj_part, jnp.pad(gram_part, ((0, 0), (0, LANES - rank)))], axis=0
    )
    joined = jnp.sum(share(joined, "z", NZ), axis=0)
    proj = joined[:rank]
    gram = joined[rank:, :rank]

    q_local = exact_dot(proj, grad_queries, (((1,), (0,)), ((), ())))
    q_flat = q_local.reshape(rank, width // LANES, LANES).transpose(1, 0, 2).reshape(-1, LANES)
    q_sum = sum_all(q_flat).reshape(width // LANES, rank, LANES).transpose(1, 0, 2)
    q_sum = q_sum.reshape(rank, width)

    lower = jnp.linalg.cholesky(gram)
    inverse = lax.linalg.triangular_solve(
        lower, jnp.eye(rank, dtype=f32), left_side=True, lower=True
    )
    p_factor = lax.dot_general(p_sum, inverse, (((0,), (1,)), ((), ())), precision=HIGHEST)
    q_factor = lax.dot_general(q_sum, inverse, (((0,), (1,)), ((), ())), precision=HIGHEST) / batch
    return (grad_queries[None], grad_passages[None], p_factor, q_factor)


def solution(mesh):
    grid = Mesh(mesh.devices.reshape(2, NY, 2, 2, NZ), ("rep", "y", "xh", "xl", "z"))
    dp = ("y", "xh", "xl")
    placed = (
        P("rep", dp, "z"),
        P("rep", dp, "z"),
        P("rep", dp),
        P("rep", dp, "z"),
        P("z", None),
    )
    return jax.shard_map(
        body,
        mesh=grid,
        in_specs=placed,
        out_specs=(P("rep", dp, "z"), P("rep", dp, "z"), P("z", None), P("z", None)),
        check_vma=False,
    )
```

```python
import math

import jax
import jax.numpy as jnp
from jax import lax
from jax.experimental import pallas as pl
from jax.experimental.pallas import tpu as pltpu
from jax.sharding import Mesh, PartitionSpec as P

LEVELS = 7
SOFTMAX_TEMP = 4.0
NY = 8
NX = 4
NZ = 8
LANES = 128
f32 = jnp.float32
bf16 = jnp.bfloat16
HIGHEST = lax.Precision.HIGHEST
VMEM = pl.BlockSpec(memory_space=pltpu.VMEM)
ANY = pl.BlockSpec(memory_space=pl.ANY)
ALL_ROWS = ("rep", "y", "xh", "xl")
NT = (((1,), (1,)), ((), ()))
TN = (((0,), (0,)), ((), ()))


def scale_of(level, full):
    return SOFTMAX_TEMP / math.sqrt(full >> level)


def swap(blocks, axes):
    return lax.all_to_all(blocks, axes, 0, 0, tiled=True)


def share(block, axes, count):
    return swap(jnp.broadcast_to(block[None], (count,) + block.shape), axes)


def query_rows(q_ref, chunk, low, high):
    return jnp.concatenate([q_ref[half, chunk, :, low:high] for half in range(2)], axis=0)


def level_scores(q_ref, raw_p_ref, p_ref, sems, finish):
    _, chunks, half_rows, width = q_ref.shape
    full = chunks * width
    piece = raw_p_ref.shape[2]
    lane = lax.broadcasted_iota(jnp.int32, (2 * half_rows, LANES), 1)
    moves = []
    for y in range(raw_p_ref.shape[0]):
        for half in range(2):
            moves.append(
                pltpu.make_async_copy(
                    raw_p_ref.at[y, pl.ds(half * chunks, chunks)],
                    p_ref.at[:, pl.ds((2 * y + half) * piece, piece)],
                    sems.at[2 * y + half],
                )
            )
    for move in moves:
        move.start()
    for move in moves:
        move.wait()

    def dot(chunk, low, high):
        return lax.dot_general(
            query_rows(q_ref, chunk, low, high), p_ref[chunk, :, low:high], NT,
            preferred_element_type=f32,
        )

    raw = None
    for level in reversed(range(LEVELS)):
        upper = full >> level
        lower = full >> (level + 1) if level + 1 < LEVELS else 0
        if upper < LANES:
            q = query_rows(q_ref, 0, 0, LANES)
            q = jnp.where(lane < upper, q, jnp.zeros_like(q))
            finish(
                level,
                lax.dot_general(q, p_ref[0, :, :LANES], NT, preferred_element_type=f32),
            )
            continue
        if upper == LANES:
            raw = dot(0, 0, LANES)
        elif upper <= width:
            raw = raw + dot(0, lower, upper)
        else:
            parts = [dot(c, 0, width) for c in range(lower // width, upper // width)]
            while len(parts) > 1:
                parts = [a + b for a, b in zip(parts[::2], parts[1::2])]
            raw = raw + parts[0]
        finish(level, raw)


def scores_kernel(q_ref, raw_p_ref, stats_ref, p_ref, table_ref, sems):
    full = q_ref.shape[1] * q_ref.shape[3]
    lane = lax.broadcasted_iota(jnp.int32, table_ref.shape, 1)
    table_ref[...] = jnp.zeros(table_ref.shape, f32)

    def finish(level, raw):
        logits = scale_of(level, full) * raw
        top = jnp.max(logits, axis=1, keepdims=True)
        total = jnp.sum(jnp.exp(logits - top), axis=1, keepdims=True)
        table_ref[...] = jnp.where(lane == level, top + jnp.log(total), table_ref[...])

    level_scores(q_ref, raw_p_ref, p_ref, sems, finish)
    stats_ref[...] = table_ref[...].T[:8]


def three_terms(value):
    hi = value.astype(bf16)
    rest = value - hi.astype(f32)
    mid = rest.astype(bf16)
    return hi, mid, (rest - mid.astype(f32)).astype(bf16)


def grads_kernel(
    at_ref, q_ref, raw_p_ref, all_ref, pos_ref, s_ref, gq_ref, gp_ref, sk_ref, p_ref, grad_ref, sems
):
    _, chunks, half_rows, width = q_ref.shape
    rows = 2 * half_rows
    full = chunks * width
    cols = p_ref.shape[1]
    rank = s_ref.shape[1]
    piece = gp_ref.shape[2]
    peak = all_ref[0]
    for src in range(1, all_ref.shape[0]):
        peak = jnp.maximum(peak, all_ref[src])
    total = jnp.exp(all_ref[0] - peak)
    for src in range(1, all_ref.shape[0]):
        total = total + jnp.exp(all_ref[src] - peak)
    joint = peak + jnp.log(total)
    place = jnp.broadcast_to(pos_ref[...].astype(f32), (8, rows))
    table = jnp.concatenate([joint, place, jnp.zeros((LANES - 16, rows), f32)], axis=0).T
    column = lax.broadcasted_iota(jnp.int32, (rows, cols), 1).astype(f32)

    def finish(level, raw):
        scale = scale_of(level, full)
        soft = jnp.exp(scale * raw - table[:, level:level + 1])
        grad_ref[level] = scale * jnp.where(column == table[:, 8:9], soft - 1.0, soft)

    level_scores(q_ref, raw_p_ref, p_ref, sems, finish)
    coef = jnp.zeros((rows, cols), f32)
    lane = lax.broadcasted_iota(jnp.int32, (1, LANES), 1)
    sk_ref[...] = jnp.zeros(sk_ref.shape, f32)

    def put(chunk, low, high, gq, gp):
        gq_hi = gq.astype(bf16)
        gq_ref[chunk, :, low:high] = gq_hi
        gp = gp.astype(bf16)
        for part in range(rows // piece):
            gp_ref[part // 2, part % 2 * chunks + chunk, :, low:high] = gp[
                part * piece:(part + 1) * piece
            ]
        gq_lo = (gq - gq_hi.astype(f32)).astype(bf16)
        terms = three_terms(s_ref[(at_ref[0] + chunks - chunk) % chunks, :, low:high])
        big = lax.dot_general(
            jnp.concatenate(terms, axis=0), gq_hi, NT, preferred_element_type=f32
        )
        low_part = lax.dot_general(
            jnp.concatenate(terms[:2], axis=0), gq_lo, NT, preferred_element_type=f32
        )
        small = big[2 * rank:] + low_part[rank:]
        sk_ref[...] += small + (big[rank:2 * rank] + low_part[:rank]) + big[:rank]

    def both(c, chunk, low, high):
        gq = jnp.dot(c, p_ref[chunk, :, low:high], preferred_element_type=f32)
        gp = lax.dot_general(
            c, query_rows(q_ref, chunk, low, high), TN, preferred_element_type=f32
        )
        return gq, gp

    held = None
    for level in range(LEVELS):
        coef = coef + grad_ref[level]
        c = coef.astype(bf16)
        upper = full >> level
        lower = full >> (level + 1) if level + 1 < LEVELS else 0
        if upper > width:
            for chunk in range(lower // width, upper // width):
                put(chunk, 0, width, *both(c, chunk, 0, width))
        elif lower >= LANES:
            put(0, lower, upper, *both(c, 0, lower, upper))
        else:
            gq, gp = both(c, 0, 0, LANES)
            if held is None:
                held = (gq, gp)
            else:
                gq = jnp.where(lane < upper, gq, held[0])
                gp = jnp.where(lane < upper, gp, held[1])
                put(0, 0, LANES, gq, gp)


def exact_dot(wide, narrow, dims):
    hi, mid, lo = [
        lax.dot_general(t, narrow, dims, preferred_element_type=f32) for t in three_terms(wide)
    ]
    return (lo + mid) + hi


def sum_scattered(value):
    count = 2 * NY * NX
    return jnp.sum(swap(value.reshape(count, -1, LANES), ALL_ROWS), axis=0)


def gathered(piece):
    return share(piece, ALL_ROWS, 2 * NY * NX).reshape(-1, LANES)


def body(queries, passages, positives, hidden_rows, sketch):
    q = queries[0]
    p = passages[0]
    rows, width = q.shape
    full = width * NZ
    rank = sketch.shape[1]
    xl = lax.axis_index("xl")
    zi = lax.axis_index("z")
    flip = [(0, 1), (1, 0)]

    piece = rows // NZ
    p_cut = jnp.broadcast_to(p.reshape(1, NZ, piece, width), (2, NZ, piece, width))
    p_cut = swap(p_cut.reshape(2 * NZ, piece, width), ("xh", "z"))
    q_blocks = jnp.broadcast_to(q[None], (2 * NZ, rows, width))
    pos_other = lax.ppermute(positives, "xl", flip)
    p_cut, q_blocks, s_own, pos_other = lax.optimization_barrier(
        (p_cut, q_blocks, sketch.T, pos_other)
    )
    p_raw = lax.all_gather(p_cut, "y")

    q_tile = swap(q_blocks, ("xl", "z")).reshape(2, NZ, rows, width)
    pos_pair = jnp.concatenate(
        [jnp.where(xl == 0, positives, pos_other), jnp.where(xl == 0, pos_other, positives)], axis=1
    )

    fetched = []
    for odd in range(2):
        pairs = []
        for r in range(2):
            for h in range(2):
                far = 2 * (2 * h + r) + odd
                at = (2 * r + h) * NZ
                pairs += [(at + i, at + (i + far) % NZ) for i in range(NZ)]
        fetched.append(lax.ppermute(s_own, ("rep", "xl", "z"), pairs))
    q_tile, p_raw, fetched = lax.optimization_barrier((q_tile, p_raw, fetched))
    tile = 2 * rows
    stats = pl.pallas_call(
        scores_kernel,
        out_shape=jax.ShapeDtypeStruct((8, tile), f32),
        in_specs=[VMEM, ANY],
        out_specs=VMEM,
        scratch_shapes=[
            pltpu.VMEM((NZ, tile, width), bf16),
            pltpu.VMEM((tile, LANES), f32),
            pltpu.SemaphoreType.DMA((2 * NY,)),
        ],
        compiler_params=pltpu.CompilerParams(vmem_limit_bytes=20 << 20),
        name="scores",
    )(q_tile, p_raw)
    stats, fetched = lax.optimization_barrier((stats, fetched))
    stats_all = share(stats, ("xl", "z"), 2 * NZ)
    s_all = jnp.stack(fetched)
    for axis in ("rep", "xl"):
        s_far = lax.ppermute(s_all, axis, flip)
        low = lax.axis_index(axis) == 0
        s_all = jnp.concatenate([jnp.where(low, s_all, s_far), jnp.where(low, s_far, s_all)])

    own_y = pos_pair // (rows * NX)
    own_x = pos_pair // rows % NX
    inside = (own_x % 2 == xl) & (pos_pair % rows // piece == zi)
    local = (own_y * 2 + own_x // 2) * piece + pos_pair % piece
    local = jnp.where(inside, local, -1)

    gq_part, gp_part, sk_part = pl.pallas_call(
        grads_kernel,
        out_shape=(
            jax.ShapeDtypeStruct((NZ, tile, width), bf16),
            jax.ShapeDtypeStruct((NY, 2 * NZ, piece, width), bf16),
            jax.ShapeDtypeStruct((rank, tile), f32),
        ),
        in_specs=[pl.BlockSpec(memory_space=pltpu.SMEM), VMEM, ANY] + [VMEM] * 3,
        out_specs=(VMEM, VMEM, VMEM),
        scratch_shapes=[
            pltpu.VMEM((NZ, tile, width), bf16),
            pltpu.VMEM((LEVELS, tile, tile), f32),
            pltpu.SemaphoreType.DMA((2 * NY,)),
        ],
        compiler_params=pltpu.CompilerParams(vmem_limit_bytes=28 << 20),
        name="grads",
    )(zi.astype(jnp.int32).reshape(1), q_tile, p_raw, stats_all, local, s_all)

    gq_sum = lax.psum_scatter(gq_part, "z", scatter_dimension=0)

    gp_sum = lax.psum_scatter(gp_part, "y", scatter_dimension=0)

    sk_blocks = jnp.stack([sk_part[:, :rows], sk_part[:, rows:]])
    sk_blocks = jnp.broadcast_to(sk_blocks[:, None], (2, NZ, rank, rows))
    sk_landed = swap(sk_blocks.reshape(2 * NZ, rank, rows), ("xl", "z"))
    batch = rows * NX * NY * 2
    sketched = jnp.sum(sk_landed, axis=0) / batch

    hidden = hidden_rows[0]
    units = hidden.shape[1]
    tiles = units // LANES
    padded = -(-tiles // 2) * 2 + (2 if tiles % 4 else 0)
    p_local = exact_dot(sketched, hidden, (((1,), (0,)), ((), ())))
    flat = p_local.reshape(rank, tiles, LANES).transpose(1, 0, 2).reshape(tiles * rank, LANES)
    pad = padded * rank - tiles * rank
    flat = jnp.concatenate([flat, jnp.zeros((pad, LANES), f32)], axis=0)
    p_flat = gathered(sum_scattered(flat))[:tiles * rank]
    p_sum = p_flat.reshape(tiles, rank, LANES).transpose(1, 0, 2).reshape(rank, units)
    gram_part = lax.dot_general(p_sum, p_sum, NT, precision=HIGHEST)
    proj_part = exact_dot(p_sum, hidden, NT)
    joined = jnp.concatenate(
        [proj_part, jnp.pad(gram_part, ((0, 0), (0, LANES - rank)))], axis=0
    )
    joined, gq_sum = lax.optimization_barrier((joined, gq_sum))
    mine = jnp.where(xl == 0, gq_sum[:rows], gq_sum[rows:])
    other = jnp.where(xl == 0, gq_sum[rows:], gq_sum[:rows])
    other = lax.ppermute(other, "xl", flip)
    grad_queries = (mine.astype(f32) + other.astype(f32)).astype(bf16)
    joined = jnp.sum(share(joined, "z", NZ), axis=0)
    proj = joined[:rank]
    gram = joined[rank:, :rank]

    q_local = exact_dot(proj, grad_queries, (((1,), (0,)), ((), ())))
    q_flat = q_local.reshape(rank, width // LANES, LANES).transpose(1, 0, 2).reshape(-1, LANES)
    q_part = sum_scattered(q_flat)
    q_part, gp_sum = lax.optimization_barrier((q_part, gp_sum))
    q_sum = gathered(q_part).reshape(width // LANES, rank, LANES).transpose(1, 0, 2)
    q_sum = q_sum.reshape(rank, width)
    keep = lax.axis_index("xh") == 0
    gp_far = lax.ppermute(jnp.where(keep, gp_sum[NZ:], gp_sum[:NZ]), "xh", flip)
    gp_near = jnp.where(keep, gp_sum[:NZ], gp_sum[NZ:])
    gp_pair = (gp_near.astype(f32) + gp_far.astype(f32)).astype(bf16)
    grad_passages = swap(gp_pair, "z").reshape(rows, width)

    lower = jnp.linalg.cholesky(gram)
    inverse = lax.linalg.triangular_solve(
        lower, jnp.eye(rank, dtype=f32), left_side=True, lower=True
    )
    p_factor = lax.dot_general(p_sum, inverse, (((0,), (1,)), ((), ())), precision=HIGHEST)
    q_factor = lax.dot_general(q_sum, inverse, (((0,), (1,)), ((), ())), precision=HIGHEST) / batch
    return (grad_queries[None], grad_passages[None], p_factor, q_factor)


def solution(mesh):
    grid = Mesh(mesh.devices.reshape(2, NY, 2, 2, NZ), ("rep", "y", "xh", "xl", "z"))
    dp = ("y", "xh", "xl")
    placed = (
        P("rep", dp, "z"),
        P("rep", dp, "z"),
        P("rep", dp),
        P("rep", dp, "z"),
        P("z", None),
    )
    return jax.shard_map(
        body,
        mesh=grid,
        in_specs=placed,
        out_specs=(P("rep", dp, "z"), P("rep", dp, "z"), P("z", None), P("z", None)),
        check_vma=False,
    )
```

```python
import math

import jax
import jax.numpy as jnp
from jax import lax
from jax.experimental import pallas as pl
from jax.experimental.pallas import tpu as pltpu
from jax.sharding import Mesh, PartitionSpec as P

LEVELS = 7
SOFTMAX_TEMP = 4.0
NY = 8
NX = 4
NZ = 8
LANES = 128
f32 = jnp.float32
bf16 = jnp.bfloat16
HIGHEST = lax.Precision.HIGHEST
VMEM = pl.BlockSpec(memory_space=pltpu.VMEM)
HBM = pl.BlockSpec(memory_space=pltpu.HBM)
ALL_ROWS = ("rep", "y", "xh", "xl")
NT = (((1,), (1,)), ((), ()))
TN = (((0,), (0,)), ((), ()))


def scale_of(level, full):
    return SOFTMAX_TEMP / math.sqrt(full >> level)


def swap(blocks, axes):
    return lax.all_to_all(blocks, axes, 0, 0, tiled=True)


def share(block, axes, count):
    return swap(jnp.broadcast_to(block[None], (count,) + block.shape), axes)


def three_terms(value):
    hi = value.astype(bf16)
    rest = value - hi.astype(f32)
    mid = rest.astype(bf16)
    return hi, mid, (rest - mid.astype(f32)).astype(bf16)


def pieces_kernel(p_ref, s_ref, out_ref):
    _, chunks, piece, _ = out_ref.shape
    width = p_ref.shape[1]
    terms = [jnp.dot(p_ref[...], t, preferred_element_type=f32) for t in three_terms(s_ref[...])]
    products = terms[2] + terms[1] + terms[0]
    hi = products.astype(bf16)
    lo = (products - hi.astype(f32)).astype(bf16)
    for half in range(2):
        for chunk in range(chunks):
            rows = slice(chunk * piece, (chunk + 1) * piece)
            out_ref[half, chunk, :, :width] = p_ref[rows]
            out_ref[half, chunk, :, width:width + LANES] = hi[rows]
            out_ref[half, chunk, :, width + LANES:] = lo[rows]


def query_rows(q_ref, chunk, low, high):
    return jnp.concatenate([q_ref[half, chunk, :, low:high] for half in range(2)], axis=0)


def level_scores(q_ref, raw_p_ref, p_ref, sems, finish):
    _, chunks, half_rows, width = q_ref.shape
    full = chunks * width
    piece = raw_p_ref.shape[2]
    lane = lax.broadcasted_iota(jnp.int32, (2 * half_rows, LANES), 1)
    moves = []
    for y in range(raw_p_ref.shape[0]):
        for half in range(2):
            moves.append(
                pltpu.make_async_copy(
                    raw_p_ref.at[y, pl.ds(half * chunks, chunks), :, pl.ds(0, p_ref.shape[2])],
                    p_ref.at[:, pl.ds((2 * y + half) * piece, piece)],
                    sems.at[2 * y + half],
                )
            )
    for move in moves:
        move.start()
    for move in moves:
        move.wait()

    def dot(chunk, low, high):
        return lax.dot_general(
            query_rows(q_ref, chunk, low, high), p_ref[chunk, :, low:high], NT,
            preferred_element_type=f32,
        )

    raw = None
    for level in reversed(range(LEVELS)):
        upper = full >> level
        lower = full >> (level + 1) if level + 1 < LEVELS else 0
        if upper < LANES:
            q = query_rows(q_ref, 0, 0, LANES)
            q = jnp.where(lane < upper, q, jnp.zeros_like(q))
            finish(
                level,
                lax.dot_general(q, p_ref[0, :, :LANES], NT, preferred_element_type=f32),
            )
            continue
        if upper == LANES:
            raw = dot(0, 0, LANES)
        elif upper <= width:
            raw = raw + dot(0, lower, upper)
        else:
            parts = [dot(c, 0, width) for c in range(lower // width, upper // width)]
            while len(parts) > 1:
                parts = [a + b for a, b in zip(parts[::2], parts[1::2])]
            raw = raw + parts[0]
        finish(level, raw)


def scores_kernel(q_ref, raw_p_ref, stats_ref, p_ref, table_ref, sems):
    full = q_ref.shape[1] * q_ref.shape[3]
    lane = lax.broadcasted_iota(jnp.int32, table_ref.shape, 1)
    table_ref[...] = jnp.zeros(table_ref.shape, f32)

    def finish(level, raw):
        logits = scale_of(level, full) * raw
        top = jnp.max(logits, axis=1, keepdims=True)
        total = jnp.sum(jnp.exp(logits - top), axis=1, keepdims=True)
        table_ref[...] = jnp.where(lane == level, top + jnp.log(total), table_ref[...])

    level_scores(q_ref, raw_p_ref, p_ref, sems, finish)
    stats_ref[...] = table_ref[...].T[:8]


def grads_kernel(
    q_ref, raw_p_ref, all_ref, pos_ref, gq_ref, gp_ref, sk_ref, p_ref, grad_ref, sems
):
    _, chunks, half_rows, width = q_ref.shape
    rows = 2 * half_rows
    full = chunks * width
    cols = p_ref.shape[1]
    rank = sk_ref.shape[0]
    piece = gp_ref.shape[2]
    peak = all_ref[0]
    for src in range(1, all_ref.shape[0]):
        peak = jnp.maximum(peak, all_ref[src])
    total = jnp.exp(all_ref[0] - peak)
    for src in range(1, all_ref.shape[0]):
        total = total + jnp.exp(all_ref[src] - peak)
    joint = peak + jnp.log(total)
    place = jnp.broadcast_to(pos_ref[...].astype(f32), (8, rows))
    table = jnp.concatenate([joint, place, jnp.zeros((LANES - 16, rows), f32)], axis=0).T
    column = lax.broadcasted_iota(jnp.int32, (rows, cols), 1).astype(f32)

    def finish(level, raw):
        scale = scale_of(level, full)
        soft = jnp.exp(scale * raw - table[:, level:level + 1])
        grad_ref[level] = scale * jnp.where(column == table[:, 8:9], soft - 1.0, soft)

    level_scores(q_ref, raw_p_ref, p_ref, sems, finish)
    coef = jnp.zeros((rows, cols), f32)
    lane = lax.broadcasted_iota(jnp.int32, (1, LANES), 1)
    sub_lane = lax.broadcasted_iota(jnp.int32, (cols, LANES), 1) // rank
    sketched = jnp.zeros((rows, LANES), f32)

    def products(chunk):
        hi = p_ref[chunk, :, width:width + LANES].astype(f32)
        return hi + p_ref[chunk, :, width + LANES:].astype(f32)

    def put(chunk, low, high, gq, gp):
        gq_ref[chunk, :, low:high] = gq.astype(bf16)
        gp = gp.astype(bf16)
        for part in range(rows // piece):
            gp_ref[part // 2, part % 2 * chunks + chunk, :, low:high] = gp[
                part * piece:(part + 1) * piece
            ]

    def both(c, chunk, low, high):
        gq = jnp.dot(c, p_ref[chunk, :, low:high], preferred_element_type=f32)
        gp = lax.dot_general(
            c, query_rows(q_ref, chunk, low, high), TN, preferred_element_type=f32
        )
        return gq, gp

    held = None
    for level in range(LEVELS):
        coef = coef + grad_ref[level]
        c = coef.astype(bf16)
        upper = full >> level
        lower = full >> (level + 1) if level + 1 < LEVELS else 0
        if upper > width:
            own = products(lower // width)
            for chunk in range(lower // width + 1, upper // width):
                own = own + products(chunk)
        else:
            own = jnp.where(sub_lane == LEVELS - 1 - level, products(0), 0.0)
        for term in three_terms(own)[::-1]:
            sketched = sketched + jnp.dot(c, term, preferred_element_type=f32)
        if upper > width:
            for chunk in range(lower // width, upper // width):
                put(chunk, 0, width, *both(c, chunk, 0, width))
        elif lower >= LANES:
            put(0, lower, upper, *both(c, 0, lower, upper))
        else:
            gq, gp = both(c, 0, 0, LANES)
            if held is None:
                held = (gq, gp)
            else:
                gq = jnp.where(lane < upper, gq, held[0])
                gp = jnp.where(lane < upper, gp, held[1])
                put(0, 0, LANES, gq, gp)
    turned = sketched.T
    total = turned[:rank]
    for sub in range(1, LANES // rank):
        total = total + turned[sub * rank:(sub + 1) * rank]
    sk_ref[...] = total


def exact_dot(wide, narrow, dims):
    hi, mid, lo = [
        lax.dot_general(t, narrow, dims, preferred_element_type=f32) for t in three_terms(wide)
    ]
    return (lo + mid) + hi


def sum_scattered(value):
    count = 2 * NY * NX
    return jnp.sum(swap(value.reshape(count, -1, LANES), ALL_ROWS), axis=0)


def gathered(piece):
    return share(piece, ALL_ROWS, 2 * NY * NX).reshape(-1, LANES)


def body(queries, passages, positives, hidden_rows, sketch):
    q = queries[0]
    p = passages[0]
    rows, width = q.shape
    full = width * NZ
    rank = sketch.shape[1]
    xl = lax.axis_index("xl")
    zi = lax.axis_index("z")
    flip = [(0, 1), (1, 0)]

    piece = rows // NZ
    row = lax.broadcasted_iota(jnp.int32, (width, LANES), 0)
    sub = lax.broadcasted_iota(jnp.int32, (width, LANES), 1) // rank
    upper = (full >> (LEVELS - 1)) << sub
    lower = jnp.where(sub == 0, 0, upper // 2)
    s_subs = jnp.where((row >= lower) & (row < upper), jnp.tile(sketch, (1, LANES // rank)), 0.0)
    wide = width + 2 * LANES
    p_cut = pl.pallas_call(
        pieces_kernel,
        out_shape=jax.ShapeDtypeStruct((2, NZ, piece, wide), bf16),
        in_specs=[VMEM, VMEM],
        out_specs=VMEM,
        compiler_params=pltpu.CompilerParams(vmem_limit_bytes=8 << 20),
        name="pieces",
    )(p, s_subs)
    p_cut = swap(p_cut.reshape(2 * NZ, piece, wide), ("xh", "z"))
    q_blocks = jnp.broadcast_to(q[None], (2 * NZ, rows, width))
    pos_other = lax.ppermute(positives, "xl", flip)
    p_cut, q_blocks, pos_other = lax.optimization_barrier((p_cut, q_blocks, pos_other))
    p_raw = lax.all_gather(p_cut, "y")

    q_tile = swap(q_blocks, ("xl", "z")).reshape(2, NZ, rows, width)
    pos_pair = jnp.concatenate(
        [jnp.where(xl == 0, positives, pos_other), jnp.where(xl == 0, pos_other, positives)], axis=1
    )

    tile = 2 * rows
    stats = pl.pallas_call(
        scores_kernel,
        out_shape=jax.ShapeDtypeStruct((8, tile), f32),
        in_specs=[VMEM, HBM],
        out_specs=VMEM,
        scratch_shapes=[
            pltpu.VMEM((NZ, tile, width), bf16),
            pltpu.VMEM((tile, LANES), f32),
            pltpu.SemaphoreType.DMA((2 * NY,)),
        ],
        compiler_params=pltpu.CompilerParams(vmem_limit_bytes=20 << 20),
        name="scores",
    )(q_tile, p_raw)
    stats_all = share(stats, ("xl", "z"), 2 * NZ)
    own_y = pos_pair // (rows * NX)
    own_x = pos_pair // rows % NX
    inside = (own_x % 2 == xl) & (pos_pair % rows // piece == zi)
    local = (own_y * 2 + own_x // 2) * piece + pos_pair % piece
    local = jnp.where(inside, local, -1)

    gq_part, gp_part, sk_part = pl.pallas_call(
        grads_kernel,
        out_shape=(
            jax.ShapeDtypeStruct((NZ, tile, width), bf16),
            jax.ShapeDtypeStruct((NY, 2 * NZ, piece, width), bf16),
            jax.ShapeDtypeStruct((rank, tile), f32),
        ),
        in_specs=[VMEM, HBM, VMEM, VMEM],
        out_specs=(VMEM, VMEM, VMEM),
        scratch_shapes=[
            pltpu.VMEM((NZ, tile, wide), bf16),
            pltpu.VMEM((LEVELS, tile, tile), f32),
            pltpu.SemaphoreType.DMA((2 * NY,)),
        ],
        compiler_params=pltpu.CompilerParams(vmem_limit_bytes=28 << 20),
        name="grads",
    )(q_tile, p_raw, stats_all, local)

    gq_sum = lax.psum_scatter(gq_part, "z", scatter_dimension=0)

    gp_sum = lax.psum_scatter(gp_part, "y", scatter_dimension=0)

    sk_blocks = jnp.stack([sk_part[:, :rows], sk_part[:, rows:]])
    sk_blocks = jnp.broadcast_to(sk_blocks[:, None], (2, NZ, rank, rows))
    sk_landed = swap(sk_blocks.reshape(2 * NZ, rank, rows), ("xl", "z"))
    batch = rows * NX * NY * 2
    sketched = jnp.sum(sk_landed, axis=0) / batch

    hidden = hidden_rows[0]
    units = hidden.shape[1]
    tiles = units // LANES
    padded = -(-tiles // 2) * 2 + (2 if tiles % 4 else 0)
    p_local = exact_dot(sketched, hidden, (((1,), (0,)), ((), ())))
    flat = p_local.reshape(rank, tiles, LANES).transpose(1, 0, 2).reshape(tiles * rank, LANES)
    pad = padded * rank - tiles * rank
    flat = jnp.concatenate([flat, jnp.zeros((pad, LANES), f32)], axis=0)
    p_flat = gathered(sum_scattered(flat))[:tiles * rank]
    p_sum = p_flat.reshape(tiles, rank, LANES).transpose(1, 0, 2).reshape(rank, units)
    gram_part = lax.dot_general(p_sum, p_sum, NT, precision=HIGHEST)
    proj_part = exact_dot(p_sum, hidden, NT)
    joined = jnp.concatenate(
        [proj_part, jnp.pad(gram_part, ((0, 0), (0, LANES - rank)))], axis=0
    )
    joined, gq_sum = lax.optimization_barrier((joined, gq_sum))
    mine = jnp.where(xl == 0, gq_sum[:rows], gq_sum[rows:])
    other = jnp.where(xl == 0, gq_sum[rows:], gq_sum[:rows])
    other = lax.ppermute(other, "xl", flip)
    grad_queries = (mine.astype(f32) + other.astype(f32)).astype(bf16)
    joined = jnp.sum(share(joined, "z", NZ), axis=0)
    proj = joined[:rank]
    gram = joined[rank:, :rank]

    q_local = exact_dot(proj, grad_queries, (((1,), (0,)), ((), ())))
    q_flat = q_local.reshape(rank, width // LANES, LANES).transpose(1, 0, 2).reshape(-1, LANES)
    q_part = sum_scattered(q_flat)
    q_part, gp_sum = lax.optimization_barrier((q_part, gp_sum))
    q_sum = gathered(q_part).reshape(width // LANES, rank, LANES).transpose(1, 0, 2)
    q_sum = q_sum.reshape(rank, width)
    keep = lax.axis_index("xh") == 0
    gp_far = lax.ppermute(jnp.where(keep, gp_sum[NZ:], gp_sum[:NZ]), "xh", flip)
    gp_near = jnp.where(keep, gp_sum[:NZ], gp_sum[NZ:])
    gp_pair = (gp_near.astype(f32) + gp_far.astype(f32)).astype(bf16)
    grad_passages = swap(gp_pair, "z").reshape(rows, width)

    lower = jnp.linalg.cholesky(gram)
    inverse = lax.linalg.triangular_solve(
        lower, jnp.eye(rank, dtype=f32), left_side=True, lower=True
    )
    p_factor = lax.dot_general(p_sum, inverse, (((0,), (1,)), ((), ())), precision=HIGHEST)
    q_factor = lax.dot_general(q_sum, inverse, (((0,), (1,)), ((), ())), precision=HIGHEST) / batch
    return (grad_queries[None], grad_passages[None], p_factor, q_factor)


def solution(mesh):
    grid = Mesh(mesh.devices.reshape(2, NY, 2, 2, NZ), ("rep", "y", "xh", "xl", "z"))
    dp = ("y", "xh", "xl")
    placed = (
        P("rep", dp, "z"),
        P("rep", dp, "z"),
        P("rep", dp),
        P("rep", dp, "z"),
        P("z", None),
    )
    return jax.shard_map(
        body,
        mesh=grid,
        in_specs=placed,
        out_specs=(P("rep", dp, "z"), P("rep", dp, "z"), P("z", None), P("z", None)),
        check_vma=False,
    )
```

```python
import math

import jax
import jax.numpy as jnp
from jax import lax
from jax.experimental import pallas as pl
from jax.experimental.pallas import tpu as pltpu
from jax.sharding import Mesh, PartitionSpec as P

LEVELS = 7
SOFTMAX_TEMP = 4.0
NY = 8
NX = 4
NZ = 8
LANES = 128
f32 = jnp.float32
bf16 = jnp.bfloat16
HIGHEST = lax.Precision.HIGHEST
VMEM = pl.BlockSpec(memory_space=pltpu.VMEM)
HBM = pl.BlockSpec(memory_space=pltpu.HBM)
ALL_ROWS = ("rep", "y", "xh", "xl")
NT = (((1,), (1,)), ((), ()))
TN = (((0,), (0,)), ((), ()))


def scale_of(level, full):
    return SOFTMAX_TEMP / math.sqrt(full >> level)


def swap(blocks, axes):
    return lax.all_to_all(blocks, axes, 0, 0, tiled=True)


def share(block, axes, count):
    return swap(jnp.broadcast_to(block[None], (count,) + block.shape), axes)


def three_terms(value):
    hi = value.astype(bf16)
    rest = value - hi.astype(f32)
    mid = rest.astype(bf16)
    return hi, mid, (rest - mid.astype(f32)).astype(bf16)


def pieces_kernel(p_ref, s_ref, out_ref):
    _, chunks, piece, _ = out_ref.shape
    width = p_ref.shape[1]
    terms = [jnp.dot(p_ref[...], t, preferred_element_type=f32) for t in three_terms(s_ref[...])]
    products = terms[2] + terms[1] + terms[0]
    hi = products.astype(bf16)
    lo = (products - hi.astype(f32)).astype(bf16)
    for half in range(2):
        for chunk in range(chunks):
            rows = slice(chunk * piece, (chunk + 1) * piece)
            out_ref[half, chunk, :, :width] = p_ref[rows]
            out_ref[half, chunk, :, width:width + LANES] = hi[rows]
            out_ref[half, chunk, :, width + LANES:] = lo[rows]


def query_rows(q_ref, chunk, low, high):
    return jnp.concatenate([q_ref[half, chunk, :, low:high] for half in range(2)], axis=0)


def level_scores(q_ref, raw_p_ref, p_ref, sems, finish):
    _, chunks, half_rows, width = q_ref.shape
    full = chunks * width
    piece = raw_p_ref.shape[2]
    lane = lax.broadcasted_iota(jnp.int32, (2 * half_rows, LANES), 1)
    moves = []
    for y in range(raw_p_ref.shape[0]):
        for half in range(2):
            moves.append(
                pltpu.make_async_copy(
                    raw_p_ref.at[y, pl.ds(half * chunks, chunks), :, pl.ds(0, p_ref.shape[2])],
                    p_ref.at[:, pl.ds((2 * y + half) * piece, piece)],
                    sems.at[2 * y + half],
                )
            )
    for move in moves:
        move.start()
    for move in moves:
        move.wait()

    def dot(chunk, low, high):
        return lax.dot_general(
            query_rows(q_ref, chunk, low, high), p_ref[chunk, :, low:high], NT,
            preferred_element_type=f32,
        )

    raw = None
    for level in reversed(range(LEVELS)):
        upper = full >> level
        lower = full >> (level + 1) if level + 1 < LEVELS else 0
        if upper < LANES:
            q = query_rows(q_ref, 0, 0, LANES)
            q = jnp.where(lane < upper, q, jnp.zeros_like(q))
            finish(
                level,
                lax.dot_general(q, p_ref[0, :, :LANES], NT, preferred_element_type=f32),
            )
            continue
        if upper == LANES:
            raw = dot(0, 0, LANES)
        elif upper <= width:
            raw = raw + dot(0, lower, upper)
        else:
            parts = [dot(c, 0, width) for c in range(lower // width, upper // width)]
            while len(parts) > 1:
                parts = [a + b for a, b in zip(parts[::2], parts[1::2])]
            raw = raw + parts[0]
        finish(level, raw)


def scores_kernel(q_ref, raw_p_ref, stats_ref, p_ref, table_ref, sems):
    full = q_ref.shape[1] * q_ref.shape[3]
    lane = lax.broadcasted_iota(jnp.int32, table_ref.shape, 1)
    table_ref[...] = jnp.zeros(table_ref.shape, f32)

    def finish(level, raw):
        logits = scale_of(level, full) * raw
        top = jnp.max(logits, axis=1, keepdims=True)
        total = jnp.sum(jnp.exp(logits - top), axis=1, keepdims=True)
        table_ref[...] = jnp.where(lane == level, top + jnp.log(total), table_ref[...])

    level_scores(q_ref, raw_p_ref, p_ref, sems, finish)
    stats_ref[...] = table_ref[...].T[:8]


def grads_kernel(
    q_ref, raw_p_ref, all_ref, pos_ref, gq_ref, gp_ref, sk_ref, p_ref, grad_ref, sems
):
    _, chunks, half_rows, width = q_ref.shape
    rows = 2 * half_rows
    full = chunks * width
    cols = p_ref.shape[1]
    rank = sk_ref.shape[0]
    piece = gp_ref.shape[2]
    peak = all_ref[0]
    for src in range(1, all_ref.shape[0]):
        peak = jnp.maximum(peak, all_ref[src])
    total = jnp.exp(all_ref[0] - peak)
    for src in range(1, all_ref.shape[0]):
        total = total + jnp.exp(all_ref[src] - peak)
    joint = peak + jnp.log(total)
    place = jnp.broadcast_to(pos_ref[...].astype(f32), (8, rows))
    table = jnp.concatenate([joint, place, jnp.zeros((LANES - 16, rows), f32)], axis=0).T
    column = lax.broadcasted_iota(jnp.int32, (rows, cols), 1).astype(f32)

    def finish(level, raw):
        scale = scale_of(level, full)
        soft = jnp.exp(scale * raw - table[:, level:level + 1])
        grad_ref[level] = scale * jnp.where(column == table[:, 8:9], soft - 1.0, soft)

    level_scores(q_ref, raw_p_ref, p_ref, sems, finish)
    coef = jnp.zeros((rows, cols), f32)
    lane = lax.broadcasted_iota(jnp.int32, (1, LANES), 1)
    sub_lane = lax.broadcasted_iota(jnp.int32, (cols, LANES), 1) // rank
    sketched = jnp.zeros((rows, LANES), f32)

    def products(chunk):
        hi = p_ref[chunk, :, width:width + LANES].astype(f32)
        return hi + p_ref[chunk, :, width + LANES:].astype(f32)

    def put(chunk, low, high, gq, gp):
        gq_ref[chunk, :, low:high] = gq.astype(bf16)
        gp = gp.astype(bf16)
        for part in range(rows // piece):
            gp_ref[part // 2, part % 2 * chunks + chunk, :, low:high] = gp[
                part * piece:(part + 1) * piece
            ]

    def both(c, chunk, low, high):
        gq = jnp.dot(c, p_ref[chunk, :, low:high], preferred_element_type=f32)
        gp = lax.dot_general(
            c, query_rows(q_ref, chunk, low, high), TN, preferred_element_type=f32
        )
        return gq, gp

    held = None
    for level in range(LEVELS):
        coef = coef + grad_ref[level]
        c = coef.astype(bf16)
        upper = full >> level
        lower = full >> (level + 1) if level + 1 < LEVELS else 0
        if upper > width:
            own = products(lower // width)
            for chunk in range(lower // width + 1, upper // width):
                own = own + products(chunk)
        else:
            own = jnp.where(sub_lane == LEVELS - 1 - level, products(0), 0.0)
        for term in three_terms(own)[::-1]:
            sketched = sketched + jnp.dot(c, term, preferred_element_type=f32)
        if upper > width:
            for chunk in range(lower // width, upper // width):
                put(chunk, 0, width, *both(c, chunk, 0, width))
        elif lower >= LANES:
            put(0, lower, upper, *both(c, 0, lower, upper))
        else:
            gq, gp = both(c, 0, 0, LANES)
            if held is None:
                held = (gq, gp)
            else:
                gq = jnp.where(lane < upper, gq, held[0])
                gp = jnp.where(lane < upper, gp, held[1])
                put(0, 0, LANES, gq, gp)
    turned = sketched.T
    total = turned[:rank]
    for sub in range(1, LANES // rank):
        total = total + turned[sub * rank:(sub + 1) * rank]
    sk_ref[...] = total


def exact_dot(wide, narrow, dims):
    hi, mid, lo = [
        lax.dot_general(t, narrow, dims, preferred_element_type=f32) for t in three_terms(wide)
    ]
    return (lo + mid) + hi


def sum_scattered(value):
    count = 2 * NY * NX
    return jnp.sum(swap(value.reshape(count, -1, LANES), ALL_ROWS), axis=0)


def gathered(piece):
    return share(piece, ALL_ROWS, 2 * NY * NX).reshape(-1, LANES)


def body(queries, passages, positives, hidden_rows, sketch):
    q = queries[0]
    p = passages[0]
    rows, width = q.shape
    full = width * NZ
    rank = sketch.shape[1]
    xl = lax.axis_index("xl")
    zi = lax.axis_index("z")
    flip = [(0, 1), (1, 0)]

    piece = rows // NZ
    row = lax.broadcasted_iota(jnp.int32, (width, LANES), 0)
    sub = lax.broadcasted_iota(jnp.int32, (width, LANES), 1) // rank
    upper = (full >> (LEVELS - 1)) << sub
    lower = jnp.where(sub == 0, 0, upper // 2)
    s_subs = jnp.where((row >= lower) & (row < upper), jnp.tile(sketch, (1, LANES // rank)), 0.0)
    wide = width + 2 * LANES
    p_cut = pl.pallas_call(
        pieces_kernel,
        out_shape=jax.ShapeDtypeStruct((2, NZ, piece, wide), bf16),
        in_specs=[VMEM, VMEM],
        out_specs=VMEM,
        compiler_params=pltpu.CompilerParams(vmem_limit_bytes=8 << 20),
        name="pieces",
    )(p, s_subs)
    p_cut = swap(p_cut.reshape(2 * NZ, piece, wide), ("xh", "z"))
    q_blocks = jnp.broadcast_to(q[None], (2 * NZ, rows, width))
    pos_other = lax.ppermute(positives, "xl", flip)
    p_cut, q_blocks, pos_other = lax.optimization_barrier((p_cut, q_blocks, pos_other))
    p_raw = lax.all_gather(p_cut, "y")

    q_tile = swap(q_blocks, ("xl", "z")).reshape(2, NZ, rows, width)
    pos_pair = jnp.concatenate(
        [jnp.where(xl == 0, positives, pos_other), jnp.where(xl == 0, pos_other, positives)], axis=1
    )

    tile = 2 * rows
    stats = pl.pallas_call(
        scores_kernel,
        out_shape=jax.ShapeDtypeStruct((8, tile), f32),
        in_specs=[VMEM, HBM],
        out_specs=VMEM,
        scratch_shapes=[
            pltpu.VMEM((NZ, tile, width), bf16),
            pltpu.VMEM((tile, LANES), f32),
            pltpu.SemaphoreType.DMA((2 * NY,)),
        ],
        compiler_params=pltpu.CompilerParams(vmem_limit_bytes=20 << 20),
        name="scores",
    )(q_tile, p_raw)
    stats_all = share(stats, ("xl", "z"), 2 * NZ)
    own_y = pos_pair // (rows * NX)
    own_x = pos_pair // rows % NX
    inside = (own_x % 2 == xl) & (pos_pair % rows // piece == zi)
    local = (own_y * 2 + own_x // 2) * piece + pos_pair % piece
    local = jnp.where(inside, local, -1)

    gq_part, gp_part, sk_part = pl.pallas_call(
        grads_kernel,
        out_shape=(
            jax.ShapeDtypeStruct((NZ, tile, width), bf16),
            jax.ShapeDtypeStruct((NY, 2 * NZ, piece, width), bf16),
            jax.ShapeDtypeStruct((rank, tile), f32),
        ),
        in_specs=[VMEM, HBM, VMEM, VMEM],
        out_specs=(VMEM, VMEM, VMEM),
        scratch_shapes=[
            pltpu.VMEM((NZ, tile, wide), bf16),
            pltpu.VMEM((LEVELS, tile, tile), f32),
            pltpu.SemaphoreType.DMA((2 * NY,)),
        ],
        compiler_params=pltpu.CompilerParams(vmem_limit_bytes=28 << 20),
        name="grads",
    )(q_tile, p_raw, stats_all, local)

    gq_sum = lax.psum_scatter(gq_part, "z", scatter_dimension=0)

    gp_sum = lax.psum_scatter(gp_part, "y", scatter_dimension=0)

    sk_blocks = jnp.stack([sk_part[:, :rows], sk_part[:, rows:]])
    sk_blocks = jnp.broadcast_to(sk_blocks[:, None], (2, NZ, rank, rows))
    sk_landed = swap(sk_blocks.reshape(2 * NZ, rank, rows), ("xl", "z"))
    batch = rows * NX * NY * 2
    sketched = jnp.sum(sk_landed, axis=0) / batch

    hidden = hidden_rows[0]
    units = hidden.shape[1]
    tiles = units // LANES
    padded = -(-tiles // 2) * 2 + (2 if tiles % 4 else 0)
    p_local = exact_dot(sketched, hidden, (((1,), (0,)), ((), ())))
    flat = p_local.reshape(rank, tiles, LANES).transpose(1, 0, 2).reshape(tiles * rank, LANES)
    pad = padded * rank - tiles * rank
    flat = jnp.concatenate([flat, jnp.zeros((pad, LANES), f32)], axis=0)
    p_flat = gathered(sum_scattered(flat))[:tiles * rank]
    p_sum = p_flat.reshape(tiles, rank, LANES).transpose(1, 0, 2).reshape(rank, units)
    gram_part = lax.dot_general(p_sum, p_sum, NT, precision=HIGHEST)
    proj_part = exact_dot(p_sum, hidden, NT)
    joined = jnp.concatenate(
        [proj_part, jnp.pad(gram_part, ((0, 0), (0, LANES - rank)))], axis=0
    )
    joined, gq_sum = lax.optimization_barrier((joined, gq_sum))
    mine = jnp.where(xl == 0, gq_sum[:rows], gq_sum[rows:])
    other = jnp.where(xl == 0, gq_sum[rows:], gq_sum[:rows])
    other = lax.ppermute(other, "xl", flip)
    grad_queries = (mine.astype(f32) + other.astype(f32)).astype(bf16)
    joined = jnp.sum(share(joined, "z", NZ), axis=0)
    proj = joined[:rank]
    gram = joined[rank:, :rank]

    q_local = exact_dot(proj, grad_queries, (((1,), (0,)), ((), ())))
    q_flat = q_local.reshape(rank, width // LANES, LANES).transpose(1, 0, 2).reshape(-1, LANES)
    q_flat, gram = lax.optimization_barrier((q_flat, gram))
    q_part = sum_scattered(q_flat)
    q_sum = gathered(q_part)
    q_sum, gp_sum = lax.optimization_barrier((q_sum, gp_sum))
    q_sum = q_sum.reshape(width // LANES, rank, LANES).transpose(1, 0, 2).reshape(rank, width)
    gp_home = swap(gp_sum, ("xh", "z")).reshape(2, rows, width).astype(f32)
    grad_passages = (gp_home[0] + gp_home[1]).astype(bf16)

    lower = jnp.linalg.cholesky(gram)
    inverse = lax.linalg.triangular_solve(
        lower, jnp.eye(rank, dtype=f32), left_side=True, lower=True
    )
    p_factor = lax.dot_general(p_sum, inverse, (((0,), (1,)), ((), ())), precision=HIGHEST)
    q_factor = lax.dot_general(q_sum, inverse, (((0,), (1,)), ((), ())), precision=HIGHEST) / batch
    return (grad_queries[None], grad_passages[None], p_factor, q_factor)


def solution(mesh):
    grid = Mesh(mesh.devices.reshape(2, NY, 2, 2, NZ), ("rep", "y", "xh", "xl", "z"))
    dp = ("y", "xh", "xl")
    placed = (
        P("rep", dp, "z"),
        P("rep", dp, "z"),
        P("rep", dp),
        P("rep", dp, "z"),
        P("z", None),
    )
    return jax.shard_map(
        body,
        mesh=grid,
        in_specs=placed,
        out_specs=(P("rep", dp, "z"), P("rep", dp, "z"), P("z", None), P("z", None)),
        check_vma=False,
    )
```

```python
import math

import jax
import jax.numpy as jnp
from jax import lax
from jax.experimental import pallas as pl
from jax.experimental.pallas import tpu as pltpu
from jax.sharding import Mesh, PartitionSpec as P

LEVELS = 7
SOFTMAX_TEMP = 4.0
NY = 8
NX = 4
NZ = 8
LANES = 128
f32 = jnp.float32
bf16 = jnp.bfloat16
HIGHEST = lax.Precision.HIGHEST
VMEM = pl.BlockSpec(memory_space=pltpu.VMEM)
ALL_ROWS = ("rep", "y", "xh", "xl")
NT = (((1,), (1,)), ((), ()))
TN = (((0,), (0,)), ((), ()))


def scale_of(level, full):
    return SOFTMAX_TEMP / math.sqrt(full >> level)


def swap(blocks, axes):
    return lax.all_to_all(blocks, axes, 0, 0, tiled=True)


def share(block, axes, count):
    return swap(jnp.broadcast_to(block[None], (count,) + block.shape), axes)


def three_terms(value):
    hi = value.astype(bf16)
    rest = value - hi.astype(f32)
    mid = rest.astype(bf16)
    return hi, mid, (rest - mid.astype(f32)).astype(bf16)


def pieces_kernel(p_ref, s_ref, out_ref):
    _, chunks, piece, _ = out_ref.shape
    width = p_ref.shape[1]
    terms = [jnp.dot(p_ref[...], t, preferred_element_type=f32) for t in three_terms(s_ref[...])]
    products = terms[2] + terms[1] + terms[0]
    hi = products.astype(bf16)
    lo = (products - hi.astype(f32)).astype(bf16)
    for half in range(2):
        for chunk in range(chunks):
            rows = slice(chunk * piece, (chunk + 1) * piece)
            out_ref[half, chunk, :, :width] = p_ref[rows]
            out_ref[half, chunk, :, width:width + LANES] = hi[rows]
            out_ref[half, chunk, :, width + LANES:] = lo[rows]


def query_rows(q_ref, chunk, low, high):
    return jnp.concatenate([q_ref[half, chunk, :, low:high] for half in range(2)], axis=0)


def passage_rows(p_ref, chunk, low, high):
    ys, places = p_ref.shape[:2]
    return jnp.concatenate(
        [
            p_ref[y, place, :, low:high]
            for y in range(ys)
            for place in (chunk, places // 2 + chunk)
        ],
        axis=0,
    )


def level_scores(q_ref, p_ref, finish):
    _, chunks, half_rows, width = q_ref.shape
    full = chunks * width
    lane = lax.broadcasted_iota(jnp.int32, (2 * half_rows, LANES), 1)
    def dot(chunk, low, high):
        return lax.dot_general(
            query_rows(q_ref, chunk, low, high), passage_rows(p_ref, chunk, low, high), NT,
            preferred_element_type=f32,
        )

    raw = None
    for level in reversed(range(LEVELS)):
        upper = full >> level
        lower = full >> (level + 1) if level + 1 < LEVELS else 0
        if upper < LANES:
            q = query_rows(q_ref, 0, 0, LANES)
            q = jnp.where(lane < upper, q, jnp.zeros_like(q))
            finish(
                level,
                lax.dot_general(
                    q, passage_rows(p_ref, 0, 0, LANES), NT, preferred_element_type=f32
                ),
            )
            continue
        if upper == LANES:
            raw = dot(0, 0, LANES)
        elif upper <= width:
            raw = raw + dot(0, lower, upper)
        else:
            parts = [dot(c, 0, width) for c in range(lower // width, upper // width)]
            while len(parts) > 1:
                parts = [a + b for a, b in zip(parts[::2], parts[1::2])]
            raw = raw + parts[0]
        finish(level, raw)


def scores_kernel(q_ref, p_ref, stats_ref, table_ref):
    full = q_ref.shape[1] * q_ref.shape[3]
    lane = lax.broadcasted_iota(jnp.int32, table_ref.shape, 1)
    table_ref[...] = jnp.zeros(table_ref.shape, f32)

    def finish(level, raw):
        logits = scale_of(level, full) * raw
        top = jnp.max(logits, axis=1, keepdims=True)
        total = jnp.sum(jnp.exp(logits - top), axis=1, keepdims=True)
        table_ref[...] = jnp.where(lane == level, top + jnp.log(total), table_ref[...])

    level_scores(q_ref, p_ref, finish)
    stats_ref[...] = table_ref[...].T[:8]


def grads_kernel(
    q_ref, p_ref, all_ref, pos_ref, gq_ref, gp_ref, sk_ref, grad_ref
):
    _, chunks, half_rows, width = q_ref.shape
    rows = 2 * half_rows
    full = chunks * width
    cols = p_ref.shape[0] * 2 * p_ref.shape[2]
    rank = sk_ref.shape[0]
    piece = gp_ref.shape[2]
    peak = all_ref[0]
    for src in range(1, all_ref.shape[0]):
        peak = jnp.maximum(peak, all_ref[src])
    total = jnp.exp(all_ref[0] - peak)
    for src in range(1, all_ref.shape[0]):
        total = total + jnp.exp(all_ref[src] - peak)
    joint = peak + jnp.log(total)
    place = jnp.broadcast_to(pos_ref[...].astype(f32), (8, rows))
    table = jnp.concatenate([joint, place, jnp.zeros((LANES - 16, rows), f32)], axis=0).T
    column = lax.broadcasted_iota(jnp.int32, (rows, cols), 1).astype(f32)

    def finish(level, raw):
        scale = scale_of(level, full)
        soft = jnp.exp(scale * raw - table[:, level:level + 1])
        grad_ref[level] = scale * jnp.where(column == table[:, 8:9], soft - 1.0, soft)

    level_scores(q_ref, p_ref, finish)
    coef = jnp.zeros((rows, cols), f32)
    lane = lax.broadcasted_iota(jnp.int32, (1, LANES), 1)
    sub_lane = lax.broadcasted_iota(jnp.int32, (cols, LANES), 1) // rank
    sketched = jnp.zeros((rows, LANES), f32)

    def products(chunk):
        both = passage_rows(p_ref, chunk, width, width + 2 * LANES).astype(f32)
        return both[:, :LANES] + both[:, LANES:]

    def put(chunk, low, high, gq, gp):
        gq_ref[chunk, :, low:high] = gq.astype(bf16)
        gp = gp.astype(bf16)
        for part in range(rows // piece):
            gp_ref[part // 2, part % 2 * chunks + chunk, :, low:high] = gp[
                part * piece:(part + 1) * piece
            ]

    def both(c, chunk, low, high):
        gq = jnp.dot(c, passage_rows(p_ref, chunk, low, high), preferred_element_type=f32)
        gp = lax.dot_general(
            c, query_rows(q_ref, chunk, low, high), TN, preferred_element_type=f32
        )
        return gq, gp

    held = None
    for level in range(LEVELS):
        coef = coef + grad_ref[level]
        c = coef.astype(bf16)
        upper = full >> level
        lower = full >> (level + 1) if level + 1 < LEVELS else 0
        if upper > width:
            own = products(lower // width)
            for chunk in range(lower // width + 1, upper // width):
                own = own + products(chunk)
        else:
            own = jnp.where(sub_lane == LEVELS - 1 - level, products(0), 0.0)
        for term in three_terms(own)[::-1]:
            sketched = sketched + jnp.dot(c, term, preferred_element_type=f32)
        if upper > width:
            for chunk in range(lower // width, upper // width):
                put(chunk, 0, width, *both(c, chunk, 0, width))
        elif lower >= LANES:
            put(0, lower, upper, *both(c, 0, lower, upper))
        else:
            gq, gp = both(c, 0, 0, LANES)
            if held is None:
                held = (gq, gp)
            else:
                gq = jnp.where(lane < upper, gq, held[0])
                gp = jnp.where(lane < upper, gp, held[1])
                put(0, 0, LANES, gq, gp)
    turned = sketched.T
    total = turned[:rank]
    for sub in range(1, LANES // rank):
        total = total + turned[sub * rank:(sub + 1) * rank]
    sk_ref[...] = total


def exact_dot(wide, narrow, dims):
    hi, mid, lo = [
        lax.dot_general(t, narrow, dims, preferred_element_type=f32) for t in three_terms(wide)
    ]
    return (lo + mid) + hi


def sum_scattered(value):
    count = 2 * NY * NX
    return jnp.sum(swap(value.reshape(count, -1, LANES), ALL_ROWS), axis=0)


def gathered(piece):
    return share(piece, ALL_ROWS, 2 * NY * NX).reshape(-1, LANES)


def body(queries, passages, positives, hidden_rows, sketch):
    q = queries[0]
    p = passages[0]
    rows, width = q.shape
    full = width * NZ
    rank = sketch.shape[1]
    xl = lax.axis_index("xl")
    zi = lax.axis_index("z")
    flip = [(0, 1), (1, 0)]

    piece = rows // NZ
    row = lax.broadcasted_iota(jnp.int32, (width, LANES), 0)
    sub = lax.broadcasted_iota(jnp.int32, (width, LANES), 1) // rank
    upper = (full >> (LEVELS - 1)) << sub
    lower = jnp.where(sub == 0, 0, upper // 2)
    s_subs = jnp.where((row >= lower) & (row < upper), jnp.tile(sketch, (1, LANES // rank)), 0.0)
    wide = width + 2 * LANES
    p_cut = pl.pallas_call(
        pieces_kernel,
        out_shape=jax.ShapeDtypeStruct((2, NZ, piece, wide), bf16),
        in_specs=[VMEM, VMEM],
        out_specs=VMEM,
        compiler_params=pltpu.CompilerParams(vmem_limit_bytes=8 << 20),
        name="pieces",
    )(p, s_subs)
    p_cut = swap(p_cut.reshape(2 * NZ, piece, wide), ("xh", "z"))
    pos_other = lax.ppermute(positives, "xl", flip)
    q_blocks = jnp.broadcast_to(q[None], (2 * NZ, rows, width))
    p_cut, q_blocks, pos_other = lax.optimization_barrier((p_cut, q_blocks, pos_other))
    p_raw = lax.all_gather(p_cut, "y")

    q_tile = swap(q_blocks, ("xl", "z")).reshape(2, NZ, rows, width)
    pos_pair = jnp.concatenate(
        [jnp.where(xl == 0, positives, pos_other), jnp.where(xl == 0, pos_other, positives)], axis=1
    )

    tile = 2 * rows
    stats = pl.pallas_call(
        scores_kernel,
        out_shape=jax.ShapeDtypeStruct((8, tile), f32),
        in_specs=[VMEM, VMEM],
        out_specs=VMEM,
        scratch_shapes=[
            pltpu.VMEM((tile, LANES), f32),
        ],
        compiler_params=pltpu.CompilerParams(vmem_limit_bytes=20 << 20),
        name="scores",
    )(q_tile, p_raw)
    stats_all = share(stats, ("xl", "z"), 2 * NZ)
    own_y = pos_pair // (rows * NX)
    own_x = pos_pair // rows % NX
    inside = (own_x % 2 == xl) & (pos_pair % rows // piece == zi)
    local = (own_y * 2 + own_x // 2) * piece + pos_pair % piece
    local = jnp.where(inside, local, -1)

    gq_part, gp_part, sk_part = pl.pallas_call(
        grads_kernel,
        out_shape=(
            jax.ShapeDtypeStruct((NZ, tile, width), bf16),
            jax.ShapeDtypeStruct((NY, 2 * NZ, piece, width), bf16),
            jax.ShapeDtypeStruct((rank, tile), f32),
        ),
        in_specs=[VMEM] * 4,
        out_specs=(VMEM, VMEM, VMEM),
        scratch_shapes=[
            pltpu.VMEM((LEVELS, tile, tile), f32),
        ],
        compiler_params=pltpu.CompilerParams(vmem_limit_bytes=28 << 20),
        name="grads",
    )(q_tile, p_raw, stats_all, local)

    gq_sum = lax.psum_scatter(gq_part, "z", scatter_dimension=0)

    gp_sum = lax.psum_scatter(gp_part, "y", scatter_dimension=0)

    sk_blocks = jnp.stack([sk_part[:, :rows], sk_part[:, rows:]])
    sk_blocks = jnp.broadcast_to(sk_blocks[:, None], (2, NZ, rank, rows))
    sk_landed = swap(sk_blocks.reshape(2 * NZ, rank, rows), ("xl", "z"))
    batch = rows * NX * NY * 2
    sketched = jnp.sum(sk_landed, axis=0) / batch

    hidden = hidden_rows[0]
    units = hidden.shape[1]
    tiles = units // LANES
    padded = -(-tiles // 2) * 2 + (2 if tiles % 4 else 0)
    p_local = exact_dot(sketched, hidden, (((1,), (0,)), ((), ())))
    flat = p_local.reshape(rank, tiles, LANES).transpose(1, 0, 2).reshape(tiles * rank, LANES)
    pad = padded * rank - tiles * rank
    flat = jnp.concatenate([flat, jnp.zeros((pad, LANES), f32)], axis=0)
    p_flat = gathered(sum_scattered(flat))[:tiles * rank]
    p_sum = p_flat.reshape(tiles, rank, LANES).transpose(1, 0, 2).reshape(rank, units)
    gram_part = lax.dot_general(p_sum, p_sum, NT, precision=HIGHEST)
    proj_part = exact_dot(p_sum, hidden, NT)
    joined = jnp.concatenate(
        [proj_part, jnp.pad(gram_part, ((0, 0), (0, LANES - rank)))], axis=0
    )
    joined, gq_sum = lax.optimization_barrier((joined, gq_sum))
    mine = jnp.where(xl == 0, gq_sum[:rows], gq_sum[rows:])
    other = jnp.where(xl == 0, gq_sum[rows:], gq_sum[:rows])
    other = lax.ppermute(other, "xl", flip)
    grad_queries = (mine.astype(f32) + other.astype(f32)).astype(bf16)
    joined = jnp.sum(share(joined, "z", NZ), axis=0)
    proj = joined[:rank]
    gram = joined[rank:, :rank]

    q_local = exact_dot(proj, grad_queries, (((1,), (0,)), ((), ())))
    q_flat = q_local.reshape(rank, width // LANES, LANES).transpose(1, 0, 2).reshape(-1, LANES)
    q_flat, gram = lax.optimization_barrier((q_flat, gram))
    q_part = sum_scattered(q_flat)
    q_sum = gathered(q_part)
    q_sum, gp_sum = lax.optimization_barrier((q_sum, gp_sum))
    q_sum = q_sum.reshape(width // LANES, rank, LANES).transpose(1, 0, 2).reshape(rank, width)
    gp_home = swap(gp_sum, ("xh", "z")).reshape(2, rows, width).astype(f32)
    grad_passages = (gp_home[0] + gp_home[1]).astype(bf16)

    lower = jnp.linalg.cholesky(gram)
    inverse = lax.linalg.triangular_solve(
        lower, jnp.eye(rank, dtype=f32), left_side=True, lower=True
    )
    p_factor = lax.dot_general(p_sum, inverse, (((0,), (1,)), ((), ())), precision=HIGHEST)
    q_factor = lax.dot_general(q_sum, inverse, (((0,), (1,)), ((), ())), precision=HIGHEST) / batch
    return (grad_queries[None], grad_passages[None], p_factor, q_factor)


def solution(mesh):
    grid = Mesh(mesh.devices.reshape(2, NY, 2, 2, NZ), ("rep", "y", "xh", "xl", "z"))
    dp = ("y", "xh", "xl")
    placed = (
        P("rep", dp, "z"),
        P("rep", dp, "z"),
        P("rep", dp),
        P("rep", dp, "z"),
        P("z", None),
    )
    return jax.shard_map(
        body,
        mesh=grid,
        in_specs=placed,
        out_specs=(P("rep", dp, "z"), P("rep", dp, "z"), P("z", None), P("z", None)),
        check_vma=False,
    )
```

```python
import math

import jax
import jax.numpy as jnp
from jax import lax
from jax.experimental import pallas as pl
from jax.experimental.pallas import tpu as pltpu
from jax.sharding import Mesh, PartitionSpec as P

LEVELS = 7
SOFTMAX_TEMP = 4.0
NY = 8
NX = 4
NZ = 8
LANES = 128
f32 = jnp.float32
bf16 = jnp.bfloat16
HIGHEST = lax.Precision.HIGHEST
VMEM = pl.BlockSpec(memory_space=pltpu.VMEM)
ALL_ROWS = ("rep", "y", "xh", "xl")
NT = (((1,), (1,)), ((), ()))
TN = (((0,), (0,)), ((), ()))


def scale_of(level, full):
    return SOFTMAX_TEMP / math.sqrt(full >> level)


def swap(blocks, axes):
    return lax.all_to_all(blocks, axes, 0, 0, tiled=True)


def share(block, axes, count):
    return swap(jnp.broadcast_to(block[None], (count,) + block.shape), axes)


def three_terms(value):
    hi = value.astype(bf16)
    rest = value - hi.astype(f32)
    mid = rest.astype(bf16)
    return hi, mid, (rest - mid.astype(f32)).astype(bf16)


def pieces_kernel(p_ref, s_ref, out_ref):
    _, chunks, piece, _ = out_ref.shape
    width = p_ref.shape[1]
    terms = [jnp.dot(p_ref[...], t, preferred_element_type=f32) for t in three_terms(s_ref[...])]
    products = terms[2] + terms[1] + terms[0]
    hi = products.astype(bf16)
    lo = (products - hi.astype(f32)).astype(bf16)
    for half in range(2):
        for chunk in range(chunks):
            rows = slice(chunk * piece, (chunk + 1) * piece)
            out_ref[half, chunk, :, :width] = p_ref[rows]
            out_ref[half, chunk, :, width:width + LANES] = hi[rows]
            out_ref[half, chunk, :, width + LANES:] = lo[rows]


def query_rows(q_ref, chunk, low, high):
    return jnp.concatenate([q_ref[half, chunk, :, low:high] for half in range(2)], axis=0)


def passage_rows(p_ref, chunk, low, high):
    ys, places = p_ref.shape[:2]
    return jnp.concatenate(
        [
            p_ref[y, place, :, low:high]
            for y in range(ys)
            for place in (chunk, places // 2 + chunk)
        ],
        axis=0,
    )


def level_scores(q_ref, p_ref, finish):
    _, chunks, half_rows, width = q_ref.shape
    full = chunks * width
    lane = lax.broadcasted_iota(jnp.int32, (2 * half_rows, LANES), 1)
    def dot(chunk, low, high):
        return lax.dot_general(
            query_rows(q_ref, chunk, low, high), passage_rows(p_ref, chunk, low, high), NT,
            preferred_element_type=f32,
        )

    raw = None
    for level in reversed(range(LEVELS)):
        upper = full >> level
        lower = full >> (level + 1) if level + 1 < LEVELS else 0
        if upper < LANES:
            q = query_rows(q_ref, 0, 0, LANES)
            q = jnp.where(lane < upper, q, jnp.zeros_like(q))
            finish(
                level,
                lax.dot_general(
                    q, passage_rows(p_ref, 0, 0, LANES), NT, preferred_element_type=f32
                ),
            )
            continue
        if upper == LANES:
            raw = dot(0, 0, LANES)
        elif upper <= width:
            raw = raw + dot(0, lower, upper)
        else:
            parts = [dot(c, 0, width) for c in range(lower // width, upper // width)]
            while len(parts) > 1:
                parts = [a + b for a, b in zip(parts[::2], parts[1::2])]
            raw = raw + parts[0]
        finish(level, raw)


def scores_kernel(q_ref, p_ref, stats_ref, table_ref):
    full = q_ref.shape[1] * q_ref.shape[3]
    lane = lax.broadcasted_iota(jnp.int32, table_ref.shape, 1)
    table_ref[...] = jnp.zeros(table_ref.shape, f32)

    def finish(level, raw):
        logits = scale_of(level, full) * raw
        top = jnp.max(logits, axis=1, keepdims=True)
        total = jnp.sum(jnp.exp(logits - top), axis=1, keepdims=True)
        table_ref[...] = jnp.where(lane == level, top + jnp.log(total), table_ref[...])

    level_scores(q_ref, p_ref, finish)
    stats_ref[...] = table_ref[...].T[:8]


def grads_kernel(
    q_ref, p_ref, all_ref, pos_ref, gq_ref, gp_ref, sk_ref, grad_ref
):
    _, chunks, half_rows, width = q_ref.shape
    rows = 2 * half_rows
    full = chunks * width
    cols = p_ref.shape[0] * 2 * p_ref.shape[2]
    rank = sk_ref.shape[0]
    piece = gp_ref.shape[2]
    peak = all_ref[0]
    for src in range(1, all_ref.shape[0]):
        peak = jnp.maximum(peak, all_ref[src])
    total = jnp.exp(all_ref[0] - peak)
    for src in range(1, all_ref.shape[0]):
        total = total + jnp.exp(all_ref[src] - peak)
    joint = peak + jnp.log(total)
    place = jnp.broadcast_to(pos_ref[...].astype(f32), (8, rows))
    table = jnp.concatenate([joint, place, jnp.zeros((LANES - 16, rows), f32)], axis=0).T
    column = lax.broadcasted_iota(jnp.int32, (rows, cols), 1).astype(f32)

    def finish(level, raw):
        scale = scale_of(level, full)
        soft = jnp.exp(scale * raw - table[:, level:level + 1])
        grad_ref[level] = scale * jnp.where(column == table[:, 8:9], soft - 1.0, soft)

    level_scores(q_ref, p_ref, finish)
    coef = jnp.zeros((rows, cols), f32)
    lane = lax.broadcasted_iota(jnp.int32, (1, LANES), 1)
    sub_lane = lax.broadcasted_iota(jnp.int32, (cols, LANES), 1) // rank
    sketched = jnp.zeros((rows, LANES), f32)

    def products(chunk):
        both = passage_rows(p_ref, chunk, width, width + 2 * LANES).astype(f32)
        return both[:, :LANES] + both[:, LANES:]

    def put(chunk, low, high, gq, gp):
        gq_ref[chunk, :, low:high] = gq.astype(bf16)
        gp = gp.astype(bf16)
        for part in range(rows // piece):
            gp_ref[part // 2, part % 2 * chunks + chunk, :, low:high] = gp[
                part * piece:(part + 1) * piece
            ]

    def both(c, chunk, low, high):
        gq = jnp.dot(c, passage_rows(p_ref, chunk, low, high), preferred_element_type=f32)
        gp = lax.dot_general(
            c, query_rows(q_ref, chunk, low, high), TN, preferred_element_type=f32
        )
        return gq, gp

    held = None
    for level in range(LEVELS):
        coef = coef + grad_ref[level]
        c = coef.astype(bf16)
        upper = full >> level
        lower = full >> (level + 1) if level + 1 < LEVELS else 0
        if upper > width:
            own = products(lower // width)
            for chunk in range(lower // width + 1, upper // width):
                own = own + products(chunk)
        else:
            own = jnp.where(sub_lane == LEVELS - 1 - level, products(0), 0.0)
        for term in three_terms(own)[::-1]:
            sketched = sketched + jnp.dot(c, term, preferred_element_type=f32)
        if upper > width:
            for chunk in range(lower // width, upper // width):
                put(chunk, 0, width, *both(c, chunk, 0, width))
        elif lower >= LANES:
            put(0, lower, upper, *both(c, 0, lower, upper))
        else:
            gq, gp = both(c, 0, 0, LANES)
            if held is None:
                held = (gq, gp)
            else:
                gq = jnp.where(lane < upper, gq, held[0])
                gp = jnp.where(lane < upper, gp, held[1])
                put(0, 0, LANES, gq, gp)
    turned = sketched.T
    total = turned[:rank]
    for sub in range(1, LANES // rank):
        total = total + turned[sub * rank:(sub + 1) * rank]
    sk_ref[...] = total


def exact_dot(wide, narrow, dims):
    rows = wide.shape[0]
    terms = jnp.concatenate(three_terms(wide), axis=0)
    out = lax.dot_general(terms, narrow, dims, preferred_element_type=f32)
    hi, mid, lo = out[:rows], out[rows:2 * rows], out[2 * rows:]
    return (lo + mid) + hi


def sum_scattered(value):
    count = 2 * NY * NX
    return jnp.sum(swap(value.reshape(count, -1, LANES), ALL_ROWS), axis=0)


def gathered(piece):
    return share(piece, ALL_ROWS, 2 * NY * NX).reshape(-1, LANES)


def body(queries, passages, positives, hidden_rows, sketch):
    q = queries[0]
    p = passages[0]
    rows, width = q.shape
    full = width * NZ
    rank = sketch.shape[1]
    xl = lax.axis_index("xl")
    zi = lax.axis_index("z")
    flip = [(0, 1), (1, 0)]

    piece = rows // NZ
    row = lax.broadcasted_iota(jnp.int32, (width, LANES), 0)
    sub = lax.broadcasted_iota(jnp.int32, (width, LANES), 1) // rank
    upper = (full >> (LEVELS - 1)) << sub
    lower = jnp.where(sub == 0, 0, upper // 2)
    s_subs = jnp.where((row >= lower) & (row < upper), jnp.tile(sketch, (1, LANES // rank)), 0.0)
    wide = width + 2 * LANES
    p_cut = pl.pallas_call(
        pieces_kernel,
        out_shape=jax.ShapeDtypeStruct((2, NZ, piece, wide), bf16),
        in_specs=[VMEM, VMEM],
        out_specs=VMEM,
        compiler_params=pltpu.CompilerParams(vmem_limit_bytes=8 << 20),
        name="pieces",
    )(p, s_subs)
    p_cut = swap(p_cut.reshape(2 * NZ, piece, wide), ("xh", "z"))
    pos_other = lax.ppermute(positives, "xl", flip)
    q_blocks = jnp.broadcast_to(q[None], (2 * NZ, rows, width))
    p_cut, q_blocks, pos_other = lax.optimization_barrier((p_cut, q_blocks, pos_other))
    p_raw = lax.all_gather(p_cut, "y")

    q_tile = swap(q_blocks, ("xl", "z")).reshape(2, NZ, rows, width)
    pos_pair = jnp.concatenate(
        [jnp.where(xl == 0, positives, pos_other), jnp.where(xl == 0, pos_other, positives)], axis=1
    )

    tile = 2 * rows
    stats = pl.pallas_call(
        scores_kernel,
        out_shape=jax.ShapeDtypeStruct((8, tile), f32),
        in_specs=[VMEM, VMEM],
        out_specs=VMEM,
        scratch_shapes=[
            pltpu.VMEM((tile, LANES), f32),
        ],
        compiler_params=pltpu.CompilerParams(vmem_limit_bytes=10 << 20),
        name="scores",
    )(q_tile, p_raw)
    stats_all = share(stats, ("xl", "z"), 2 * NZ)
    own_y = pos_pair // (rows * NX)
    own_x = pos_pair // rows % NX
    inside = (own_x % 2 == xl) & (pos_pair % rows // piece == zi)
    local = (own_y * 2 + own_x // 2) * piece + pos_pair % piece
    local = jnp.where(inside, local, -1)

    gq_part, gp_part, sk_part = pl.pallas_call(
        grads_kernel,
        out_shape=(
            jax.ShapeDtypeStruct((NZ, tile, width), bf16),
            jax.ShapeDtypeStruct((NY, 2 * NZ, piece, width), bf16),
            jax.ShapeDtypeStruct((rank, tile), f32),
        ),
        in_specs=[VMEM] * 4,
        out_specs=(VMEM, VMEM, VMEM),
        scratch_shapes=[
            pltpu.VMEM((LEVELS, tile, tile), f32),
        ],
        compiler_params=pltpu.CompilerParams(vmem_limit_bytes=14 << 20),
        name="grads",
    )(q_tile, p_raw, stats_all, local)

    gq_sum = lax.psum_scatter(gq_part, "z", scatter_dimension=0)

    gp_sum = lax.psum_scatter(gp_part, "y", scatter_dimension=0)

    sk_blocks = jnp.stack([sk_part[:, :rows], sk_part[:, rows:]])
    sk_blocks = jnp.broadcast_to(sk_blocks[:, None], (2, NZ, rank, rows))
    sk_landed = swap(sk_blocks.reshape(2 * NZ, rank, rows), ("xl", "z"))
    batch = rows * NX * NY * 2
    sketched = jnp.sum(sk_landed, axis=0) / batch

    hidden = hidden_rows[0]
    units = hidden.shape[1]
    tiles = units // LANES
    padded = -(-tiles // 2) * 2 + (2 if tiles % 4 else 0)
    p_local = exact_dot(sketched, hidden, (((1,), (0,)), ((), ())))
    flat = p_local.reshape(rank, tiles, LANES).transpose(1, 0, 2).reshape(tiles * rank, LANES)
    pad = padded * rank - tiles * rank
    flat = jnp.concatenate([flat, jnp.zeros((pad, LANES), f32)], axis=0)
    p_flat = gathered(sum_scattered(flat))[:tiles * rank]
    p_sum = p_flat.reshape(tiles, rank, LANES).transpose(1, 0, 2).reshape(rank, units)
    gram_part = lax.dot_general(p_sum, p_sum, NT, precision=HIGHEST)
    proj_part = exact_dot(p_sum, hidden, NT)
    joined = jnp.concatenate(
        [proj_part, jnp.pad(gram_part, ((0, 0), (0, LANES - rank)))], axis=0
    )
    joined, gq_sum = lax.optimization_barrier((joined, gq_sum))
    mine = jnp.where(xl == 0, gq_sum[:rows], gq_sum[rows:])
    other = jnp.where(xl == 0, gq_sum[rows:], gq_sum[:rows])
    other = lax.ppermute(other, "xl", flip)
    grad_queries = (mine.astype(f32) + other.astype(f32)).astype(bf16)
    joined = jnp.sum(share(joined, "z", NZ), axis=0)
    proj = joined[:rank]
    gram = joined[rank:, :rank]

    q_local = exact_dot(proj, grad_queries, (((1,), (0,)), ((), ())))
    q_flat = q_local.reshape(rank, width // LANES, LANES).transpose(1, 0, 2).reshape(-1, LANES)
    q_flat, gram = lax.optimization_barrier((q_flat, gram))
    q_part = sum_scattered(q_flat)
    q_sum = gathered(q_part)
    q_sum, gp_sum = lax.optimization_barrier((q_sum, gp_sum))
    q_sum = q_sum.reshape(width // LANES, rank, LANES).transpose(1, 0, 2).reshape(rank, width)
    gp_home = swap(gp_sum, ("xh", "z")).reshape(2, rows, width).astype(f32)
    grad_passages = (gp_home[0] + gp_home[1]).astype(bf16)

    lower = jnp.linalg.cholesky(gram)
    inverse = lax.linalg.triangular_solve(
        lower, jnp.eye(rank, dtype=f32), left_side=True, lower=True
    )
    p_factor = lax.dot_general(p_sum, inverse, (((0,), (1,)), ((), ())), precision=HIGHEST)
    q_factor = lax.dot_general(q_sum, inverse, (((0,), (1,)), ((), ())), precision=HIGHEST) / batch
    return (grad_queries[None], grad_passages[None], p_factor, q_factor)


def solution(mesh):
    grid = Mesh(mesh.devices.reshape(2, NY, 2, 2, NZ), ("rep", "y", "xh", "xl", "z"))
    dp = ("y", "xh", "xl")
    placed = (
        P("rep", dp, "z"),
        P("rep", dp, "z"),
        P("rep", dp),
        P("rep", dp, "z"),
        P("z", None),
    )
    return jax.shard_map(
        body,
        mesh=grid,
        in_specs=placed,
        out_specs=(P("rep", dp, "z"), P("rep", dp, "z"), P("z", None), P("z", None)),
        check_vma=False,
    )
```

```python
import math

import jax
import jax.numpy as jnp
from jax import lax
from jax.experimental import pallas as pl
from jax.experimental.pallas import tpu as pltpu
from jax.sharding import Mesh, PartitionSpec as P

LEVELS = 7
SOFTMAX_TEMP = 4.0
NY = 8
NX = 4
NZ = 8
LANES = 128
f32 = jnp.float32
bf16 = jnp.bfloat16
HIGHEST = lax.Precision.HIGHEST
VMEM = pl.BlockSpec(memory_space=pltpu.VMEM)
ALL_ROWS = ("rep", "y", "xh", "xl")
NT = (((1,), (1,)), ((), ()))
TN = (((0,), (0,)), ((), ()))


def scale_of(level, full):
    return SOFTMAX_TEMP / math.sqrt(full >> level)


def swap(blocks, axes):
    return lax.all_to_all(blocks, axes, 0, 0, tiled=True)


def share(block, axes, count):
    return swap(jnp.broadcast_to(block[None], (count,) + block.shape), axes)


def three_terms(value):
    hi = value.astype(bf16)
    rest = value - hi.astype(f32)
    mid = rest.astype(bf16)
    return hi, mid, (rest - mid.astype(f32)).astype(bf16)


def pieces_kernel(p_ref, s_ref, out_ref):
    _, chunks, piece, _ = out_ref.shape
    width = p_ref.shape[1]
    terms = [jnp.dot(p_ref[...], t, preferred_element_type=f32) for t in three_terms(s_ref[...])]
    products = terms[2] + terms[1] + terms[0]
    hi = products.astype(bf16)
    lo = (products - hi.astype(f32)).astype(bf16)
    for half in range(2):
        for chunk in range(chunks):
            rows = slice(chunk * piece, (chunk + 1) * piece)
            out_ref[half, chunk, :, :width] = p_ref[rows]
            out_ref[half, chunk, :, width:width + LANES] = hi[rows]
            out_ref[half, chunk, :, width + LANES:] = lo[rows]


def query_rows(q_ref, chunk, low, high):
    return jnp.concatenate([q_ref[half, chunk, :, low:high] for half in range(2)], axis=0)


def passage_rows(p_ref, chunk, low, high):
    ys, places = p_ref.shape[:2]
    return jnp.concatenate(
        [
            p_ref[y, place, :, low:high]
            for y in range(ys)
            for place in (chunk, places // 2 + chunk)
        ],
        axis=0,
    )


def level_scores(q_ref, p_ref, finish):
    _, chunks, half_rows, width = q_ref.shape
    full = chunks * width
    lane = lax.broadcasted_iota(jnp.int32, (2 * half_rows, LANES), 1)
    def dot(chunk, low, high):
        return lax.dot_general(
            query_rows(q_ref, chunk, low, high), passage_rows(p_ref, chunk, low, high), NT,
            preferred_element_type=f32,
        )

    raw = None
    for level in reversed(range(LEVELS)):
        upper = full >> level
        lower = full >> (level + 1) if level + 1 < LEVELS else 0
        if upper < LANES:
            q = query_rows(q_ref, 0, 0, LANES)
            q = jnp.where(lane < upper, q, jnp.zeros_like(q))
            finish(
                level,
                lax.dot_general(
                    q, passage_rows(p_ref, 0, 0, LANES), NT, preferred_element_type=f32
                ),
            )
            continue
        if upper == LANES:
            raw = dot(0, 0, LANES)
        elif upper <= width:
            raw = raw + dot(0, lower, upper)
        else:
            parts = [dot(c, 0, width) for c in range(lower // width, upper // width)]
            while len(parts) > 1:
                parts = [a + b for a, b in zip(parts[::2], parts[1::2])]
            raw = raw + parts[0]
        finish(level, raw)


def scores_kernel(q_ref, p_ref, stats_ref, table_ref):
    full = q_ref.shape[1] * q_ref.shape[3]
    lane = lax.broadcasted_iota(jnp.int32, table_ref.shape, 1)
    table_ref[...] = jnp.zeros(table_ref.shape, f32)

    def finish(level, raw):
        logits = scale_of(level, full) * raw
        top = jnp.max(logits, axis=1, keepdims=True)
        total = jnp.sum(jnp.exp(logits - top), axis=1, keepdims=True)
        table_ref[...] = jnp.where(lane == level, top + jnp.log(total), table_ref[...])

    level_scores(q_ref, p_ref, finish)
    stats_ref[...] = table_ref[...].T[:8]


def grads_kernel(
    q_ref, p_ref, all_ref, pos_ref, gq_ref, gp_ref, sk_ref, grad_ref
):
    _, chunks, half_rows, width = q_ref.shape
    rows = 2 * half_rows
    full = chunks * width
    cols = p_ref.shape[0] * 2 * p_ref.shape[2]
    rank = sk_ref.shape[0]
    piece = gp_ref.shape[2]
    peak = all_ref[0]
    for src in range(1, all_ref.shape[0]):
        peak = jnp.maximum(peak, all_ref[src])
    total = jnp.exp(all_ref[0] - peak)
    for src in range(1, all_ref.shape[0]):
        total = total + jnp.exp(all_ref[src] - peak)
    joint = peak + jnp.log(total)
    place = jnp.broadcast_to(pos_ref[...].astype(f32), (8, rows))
    table = jnp.concatenate([joint, place, jnp.zeros((LANES - 16, rows), f32)], axis=0).T
    column = lax.broadcasted_iota(jnp.int32, (rows, cols), 1).astype(f32)

    def finish(level, raw):
        scale = scale_of(level, full)
        soft = jnp.exp(scale * raw - table[:, level:level + 1])
        grad_ref[level] = scale * jnp.where(column == table[:, 8:9], soft - 1.0, soft)

    level_scores(q_ref, p_ref, finish)
    coef = jnp.zeros((rows, cols), f32)
    lane = lax.broadcasted_iota(jnp.int32, (1, LANES), 1)
    sub_lane = lax.broadcasted_iota(jnp.int32, (cols, LANES), 1) // rank
    sketched = jnp.zeros((rows, LANES), f32)

    def products(chunk):
        both = passage_rows(p_ref, chunk, width, width + 2 * LANES).astype(f32)
        return both[:, :LANES] + both[:, LANES:]

    def put(chunk, low, high, gq, gp):
        gq_ref[chunk, :, low:high] = gq.astype(bf16)
        gp = gp.astype(bf16)
        for part in range(rows // piece):
            gp_ref[part // 2, part % 2 * chunks + chunk, :, low:high] = gp[
                part * piece:(part + 1) * piece
            ]

    def both(c, chunk, low, high):
        gq = jnp.dot(c, passage_rows(p_ref, chunk, low, high), preferred_element_type=f32)
        gp = lax.dot_general(
            c, query_rows(q_ref, chunk, low, high), TN, preferred_element_type=f32
        )
        return gq, gp

    held = None
    for level in range(LEVELS):
        coef = coef + grad_ref[level]
        c = coef.astype(bf16)
        upper = full >> level
        lower = full >> (level + 1) if level + 1 < LEVELS else 0
        if upper > width:
            own = products(lower // width)
            for chunk in range(lower // width + 1, upper // width):
                own = own + products(chunk)
        else:
            own = jnp.where(sub_lane == LEVELS - 1 - level, products(0), 0.0)
        for term in three_terms(own)[::-1]:
            sketched = sketched + jnp.dot(c, term, preferred_element_type=f32)
        if upper > width:
            for chunk in range(lower // width, upper // width):
                put(chunk, 0, width, *both(c, chunk, 0, width))
        elif lower >= LANES:
            put(0, lower, upper, *both(c, 0, lower, upper))
        else:
            gq, gp = both(c, 0, 0, LANES)
            if held is None:
                held = (gq, gp)
            else:
                gq = jnp.where(lane < upper, gq, held[0])
                gp = jnp.where(lane < upper, gp, held[1])
                put(0, 0, LANES, gq, gp)
    turned = sketched.T
    total = turned[:rank]
    for sub in range(1, LANES // rank):
        total = total + turned[sub * rank:(sub + 1) * rank]
    sk_ref[...] = total


def exact_dot(wide, narrow, dims):
    rows = wide.shape[0]
    terms = jnp.concatenate(three_terms(wide), axis=0)
    out = lax.dot_general(terms, narrow, dims, preferred_element_type=f32)
    hi, mid, lo = out[:rows], out[rows:2 * rows], out[2 * rows:]
    return (lo + mid) + hi


def sum_scattered(value):
    count = 2 * NY * NX
    return jnp.sum(swap(value.reshape(count, -1, LANES), ALL_ROWS), axis=0)


def gathered(piece):
    return share(piece, ALL_ROWS, 2 * NY * NX).reshape(-1, LANES)


def body(queries, passages, positives, hidden_rows, sketch):
    q = queries[0]
    p = passages[0]
    rows, width = q.shape
    full = width * NZ
    rank = sketch.shape[1]
    xl = lax.axis_index("xl")
    zi = lax.axis_index("z")
    flip = [(0, 1), (1, 0)]

    piece = rows // NZ
    row = lax.broadcasted_iota(jnp.int32, (width, LANES), 0)
    sub = lax.broadcasted_iota(jnp.int32, (width, LANES), 1) // rank
    upper = (full >> (LEVELS - 1)) << sub
    lower = jnp.where(sub == 0, 0, upper // 2)
    s_subs = jnp.where((row >= lower) & (row < upper), jnp.tile(sketch, (1, LANES // rank)), 0.0)
    wide = width + 2 * LANES
    p_cut = pl.pallas_call(
        pieces_kernel,
        out_shape=jax.ShapeDtypeStruct((2, NZ, piece, wide), bf16),
        in_specs=[VMEM, VMEM],
        out_specs=VMEM,
        compiler_params=pltpu.CompilerParams(vmem_limit_bytes=8 << 20),
        name="pieces",
    )(p, s_subs)
    p_cut = swap(p_cut.reshape(2 * NZ, piece, wide), ("xh", "z"))
    pos_other = lax.ppermute(positives, "xl", flip)
    q_blocks = jnp.broadcast_to(q[None], (2 * NZ, rows, width))
    p_cut, q_blocks, pos_other = lax.optimization_barrier((p_cut, q_blocks, pos_other))
    p_raw = lax.all_gather(p_cut, "y")

    q_tile = swap(q_blocks, ("xl", "z")).reshape(2, NZ, rows, width)
    pos_pair = jnp.concatenate(
        [jnp.where(xl == 0, positives, pos_other), jnp.where(xl == 0, pos_other, positives)], axis=1
    )

    tile = 2 * rows
    stats = pl.pallas_call(
        scores_kernel,
        out_shape=jax.ShapeDtypeStruct((8, tile), f32),
        in_specs=[VMEM, VMEM],
        out_specs=VMEM,
        scratch_shapes=[
            pltpu.VMEM((tile, LANES), f32),
        ],
        compiler_params=pltpu.CompilerParams(vmem_limit_bytes=10 << 20),
        name="scores",
    )(q_tile, p_raw)
    stats_all = share(stats, ("xl", "z"), 2 * NZ)
    own_y = pos_pair // (rows * NX)
    own_x = pos_pair // rows % NX
    inside = (own_x % 2 == xl) & (pos_pair % rows // piece == zi)
    local = (own_y * 2 + own_x // 2) * piece + pos_pair % piece
    local = jnp.where(inside, local, -1)

    gq_part, gp_part, sk_part = pl.pallas_call(
        grads_kernel,
        out_shape=(
            jax.ShapeDtypeStruct((NZ, tile, width), bf16),
            jax.ShapeDtypeStruct((NY, 2 * NZ, piece, width), bf16),
            jax.ShapeDtypeStruct((rank, tile), f32),
        ),
        in_specs=[VMEM] * 4,
        out_specs=(VMEM, VMEM, VMEM),
        scratch_shapes=[
            pltpu.VMEM((LEVELS, tile, tile), f32),
        ],
        compiler_params=pltpu.CompilerParams(vmem_limit_bytes=14 << 20),
        name="grads",
    )(q_tile, p_raw, stats_all, local)

    gq_sum = lax.psum_scatter(gq_part, "z", scatter_dimension=0)

    gp_sum = lax.psum_scatter(gp_part, "y", scatter_dimension=0)

    sk_blocks = jnp.stack([sk_part[:, :rows], sk_part[:, rows:]])
    sk_blocks = jnp.broadcast_to(sk_blocks[:, None], (2, NZ, rank, rows))
    sk_landed = swap(sk_blocks.reshape(2 * NZ, rank, rows), ("xl", "z"))
    batch = rows * NX * NY * 2
    sketched = jnp.sum(sk_landed, axis=0) / batch

    hidden = hidden_rows[0]
    units = hidden.shape[1]
    tiles = units // LANES
    padded = -(-tiles // 2) * 2 + (2 if tiles % 4 else 0)
    p_local = exact_dot(sketched, hidden, (((1,), (0,)), ((), ())))
    pad = padded * rank - tiles * rank
    flat = jnp.concatenate(
        [p_local[:, t * LANES:(t + 1) * LANES] for t in range(tiles)]
        + [jnp.zeros((pad, LANES), f32)],
        axis=0,
    )
    p_flat = gathered(sum_scattered(flat))[:tiles * rank]
    p_sum = p_flat.reshape(tiles, rank, LANES).transpose(1, 0, 2).reshape(rank, units)
    gram_part = lax.dot_general(p_sum, p_sum, NT, precision=HIGHEST)
    proj_part = exact_dot(p_sum, hidden, NT)
    joined = jnp.concatenate(
        [proj_part, jnp.pad(gram_part, ((0, 0), (0, LANES - rank)))], axis=0
    )
    joined, gq_sum = lax.optimization_barrier((joined, gq_sum))
    mine = jnp.where(xl == 0, gq_sum[:rows], gq_sum[rows:])
    other = jnp.where(xl == 0, gq_sum[rows:], gq_sum[:rows])
    other = lax.ppermute(other, "xl", flip)
    grad_queries = (mine.astype(f32) + other.astype(f32)).astype(bf16)
    joined = jnp.sum(share(joined, "z", NZ), axis=0)
    proj = joined[:rank]
    gram = joined[rank:, :rank]

    q_local = exact_dot(proj, grad_queries, (((1,), (0,)), ((), ())))
    q_flat = jnp.concatenate(
        [q_local[:, t * LANES:(t + 1) * LANES] for t in range(width // LANES)], axis=0
    )
    q_flat, gram = lax.optimization_barrier((q_flat, gram))
    q_part = sum_scattered(q_flat)
    q_sum = gathered(q_part)
    q_sum, gp_sum = lax.optimization_barrier((q_sum, gp_sum))
    q_sum = q_sum.reshape(width // LANES, rank, LANES).transpose(1, 0, 2).reshape(rank, width)
    gp_home = swap(gp_sum, ("xh", "z")).reshape(2, rows, width).astype(f32)
    grad_passages = (gp_home[0] + gp_home[1]).astype(bf16)

    lower = jnp.linalg.cholesky(gram)
    inverse = lax.linalg.triangular_solve(
        lower, jnp.eye(rank, dtype=f32), left_side=True, lower=True
    )
    p_factor = lax.dot_general(p_sum, inverse, (((0,), (1,)), ((), ())), precision=HIGHEST)
    q_factor = lax.dot_general(q_sum, inverse, (((0,), (1,)), ((), ())), precision=HIGHEST) / batch
    return (grad_queries[None], grad_passages[None], p_factor, q_factor)


def solution(mesh):
    grid = Mesh(mesh.devices.reshape(2, NY, 2, 2, NZ), ("rep", "y", "xh", "xl", "z"))
    dp = ("y", "xh", "xl")
    placed = (
        P("rep", dp, "z"),
        P("rep", dp, "z"),
        P("rep", dp),
        P("rep", dp, "z"),
        P("z", None),
    )
    return jax.shard_map(
        body,
        mesh=grid,
        in_specs=placed,
        out_specs=(P("rep", dp, "z"), P("rep", dp, "z"), P("z", None), P("z", None)),
        check_vma=False,
    )
```
